32 devices in a mesh: groups: 2 (over y), win: 4 (over z), samp: 2 (over x), head: 2 (over core).
Axes of the slice: x: 2, y: 2, z: 4, core: 2. Of those that a mesh axis runs over, the one named last changes fastest.
Arguments:
- queries: bfloat16 [4, 512, 1280], P(('groups', 'samp'), 'win', 'head'), parts along dimension 0, may hold values from -8 to 8
- key_vectors: bfloat16 [4, 512, 1280], P(('groups', 'samp'), 'win', 'head'), parts along dimension 0, may hold values from -8 to 8
- value_vectors: bfloat16 [4, 512, 1280], P(('groups', 'samp'), 'win', 'head'), parts along dimension 0, may hold values from -6 to 6
- out_grad: bfloat16 [4, 512, 1280], P(('groups', 'samp'), 'win', 'head'), parts along dimension 0, may hold values from -6 to 6
- keep_mask: int32 [4, 512], P(('groups', 'samp'), 'win'), parts along dimension 0, may hold values from 0 to 1, as said below
Outputs:
- attended: bfloat16 [4, 512, 1280], P(('groups', 'samp'), 'win', 'head'), parts along dimension 0
- grad_queries: bfloat16 [4, 512, 1280], P(('groups', 'samp'), 'win', 'head'), parts along dimension 0
- grad_keys: bfloat16 [4, 512, 1280], P(('groups', 'samp'), 'win', 'head'), parts along dimension 0
- grad_values: bfloat16 [4, 512, 1280], P(('groups', 'samp'), 'win', 'head'), parts along dimension 0
The draws below stay inside these ranges and needn't reach their ends.
There are 2 independent parts, one for each index of `groups`. The reference program is written for one: setup_inputs(seed, part) draws one part's arguments, and reference() takes and returns one part's arrays. A program takes and returns all parts, laid end to end along the dimension named above; each array names one. Nothing has to cross between parts.
Inputs may be any that keep to these rules, and one draw needn't show every extreme that they name: `keep_mask`: in every sample exactly 256 of the 512 tokens are kept (1) and the others dropped (0); in every sample the 128 tokens of some one index of win are all kept.
All inputs are finite; a program needn't handle non-finite values.
Results may differ from the reference program's by a relative error of at most 0.03.
Values may be sent and summed in bfloat16 or wider, within the bound.
No kernel may reach another device: no remote copies, remote signals or barrier semaphores. Data moves between devices by JAX's collectives and lax.ppermute only.
A program may use at most 64 MiB of HBM per device.

```python
import math
import jax
import jax.numpy as jnp
from jax import lax

HEADS = 10
HEAD_DIM = 128
TOK_DEV = 128
TOKENS = 512
KEPT = 256
SAMPLES = 2
FEAT = 1280


def kept_table(key):
    key = jax.random.fold_in(key, 101)
    key_level, key_full, key_jitter = jax.random.split(key, 3)
    win_total = TOKENS // TOK_DEV
    levels = jax.random.randint(key_level, (SAMPLES, win_total), 0, 3) * TOK_DEV
    chosen = jax.random.randint(key_full, (SAMPLES, 1), 0, win_total)
    window_bias = jnp.where(jnp.arange(win_total)[None, :] == chosen, 10 * TOK_DEV, levels)
    jitter = jax.random.randint(key_jitter, (SAMPLES, TOKENS), 0, 2 * TOK_DEV)
    scores = (jnp.repeat(window_bias, TOK_DEV, axis=1) + jitter) * TOKENS + jnp.arange(TOKENS)[None, :]
    placing = jnp.argsort(jnp.argsort(-scores, axis=1), axis=1)
    return (placing < KEPT).astype(jnp.int32)


def draw_keep_mask(key, part):
    return kept_table(key)


def draw_queries(key, part):
    key = jax.random.fold_in(key, 7)
    extent = (SAMPLES, TOKENS, HEADS * HEAD_DIM)
    return jnp.clip(1.6 * jax.random.normal(key, extent, jnp.float32), -8.0, 8.0).astype(jnp.bfloat16)


def draw_key_vectors(key, part):
    key = jax.random.fold_in(key, 9)
    extent = (SAMPLES, TOKENS, HEADS * HEAD_DIM)
    return jnp.clip(1.6 * jax.random.normal(key, extent, jnp.float32), -8.0, 8.0).astype(jnp.bfloat16)


def shard_levels(rng, shape, cuts, low, top_value):
    def one(dim, shards_of):
        steps = jax.random.uniform(jax.random.fold_in(jax.random.fold_in(rng, 6), dim), (shards_of,), jnp.float32, low / len(cuts), top_value / len(cuts))
        return jnp.repeat(jnp.exp(steps), shape[dim] // shards_of).reshape((-1,) + (1,) * (len(shape) - dim - 1))

    gain = one(*cuts[0])
    for cut in cuts[1:]:
        gain = gain * one(*cut)
    return gain


def bell_draw(own_key, dims, width, bound, cuts=(), held_as=jnp.bfloat16):
    level = shard_levels(own_key, dims, cuts, -0.22, 0.18) if cuts else 1.0
    values = jax.random.normal(own_key, dims, jnp.float32) * width * level
    return jnp.minimum(jnp.maximum(values, -bound), bound).astype(held_as)


def setup_inputs(seed: int = 0, part: int = 0) -> dict:
    seeds = jax.random.split(jax.random.key(seed), 6)
    own_keys = jax.random.split(jax.random.fold_in(seeds[5], part), 6)
    return {
        "queries": draw_queries(jax.random.fold_in(jax.random.fold_in(seeds[5], part), 71), part),
        "key_vectors": draw_key_vectors(jax.random.fold_in(jax.random.fold_in(seeds[5], part), 71), part),
        "value_vectors": bell_draw(own_keys[2], (SAMPLES, TOKENS, FEAT), 1.0, 6.0, ((0, 2), (1, 4), (2, 2))),
        "out_grad": bell_draw(own_keys[3], (SAMPLES, TOKENS, FEAT), 1.0, 6.0, ((0, 2), (1, 4), (2, 2))),
        "keep_mask": draw_keep_mask(jax.random.fold_in(jax.random.fold_in(seeds[5], part), 71), part),
    }


def attend_head(inputs):
    query_head, key_head, value_head, grad_head = inputs
    inv_root = 1.0 / math.sqrt(HEAD_DIM)
    scores = jnp.dot(query_head, key_head.T, preferred_element_type=jnp.float32) * inv_root
    highest = lax.optimization_barrier(jnp.max(scores, axis=-1, keepdims=True))
    raised = jnp.exp(scores - highest)
    totals = lax.optimization_barrier(jnp.sum(raised, axis=-1, keepdims=True))
    attended = (jnp.dot(raised.astype(jnp.bfloat16), value_head, preferred_element_type=jnp.float32) / totals).astype(jnp.bfloat16)
    log_total = highest + jnp.log(totals)
    weights = jnp.exp(scores - log_total).astype(jnp.bfloat16)
    inner = lax.optimization_barrier(jnp.sum(grad_head.astype(jnp.float32) * attended.astype(jnp.float32), axis=-1, keepdims=True))
    grad_scores = jnp.dot(grad_head, value_head.T, preferred_element_type=jnp.float32)
    grad_logits = (weights.astype(jnp.float32) * (grad_scores - inner) * inv_root).astype(jnp.bfloat16)
    grad_query = jnp.dot(grad_logits, key_head, preferred_element_type=jnp.float32).astype(jnp.bfloat16)
    grad_key = jnp.dot(grad_logits.T, query_head, preferred_element_type=jnp.float32).astype(jnp.bfloat16)
    grad_value = jnp.dot(weights.T, grad_head, preferred_element_type=jnp.float32).astype(jnp.bfloat16)
    return (attended, grad_query, grad_key, grad_value)

def attend_sample(inputs):
    queries, key_vectors, value_vectors, out_grad, keep_mask = inputs
    kept_pos = jnp.argsort(1 - keep_mask, stable=True)[:KEPT].astype(jnp.int32)

    def heads_first(matrix):
        return matrix[kept_pos].reshape(KEPT, HEADS, HEAD_DIM).transpose(1, 0, 2)
    results = lax.map(attend_head, (heads_first(queries), heads_first(key_vectors), heads_first(value_vectors), heads_first(out_grad)))
    outputs = []
    for result in results:
        flat = result.transpose(1, 0, 2).reshape(KEPT, HEADS * HEAD_DIM)
        outputs.append(jnp.zeros((TOKENS, HEADS * HEAD_DIM), flat.dtype).at[kept_pos].set(flat))
    return tuple(outputs)

def reference(queries, key_vectors, value_vectors, out_grad, keep_mask):
    attended, grad_queries, grad_keys, grad_values = lax.map(attend_sample, (queries, key_vectors, value_vectors, out_grad, keep_mask))
    return (attended, grad_queries, grad_keys, grad_values)
```

```python
import functools
import math

import jax
import jax.numpy as jnp
from jax import lax
from jax.experimental import pallas as pl
from jax.experimental.pallas import tpu as pltpu
from jax.sharding import PartitionSpec as P

HEAD_DIM = 128
MASK_ROWS = 16
QUAD = 4 * HEAD_DIM
BF16 = jnp.bfloat16
F32 = jnp.float32


def dot(left, right, left_dim=1, right_dim=0):
    return lax.dot_general(
        left, right, (((left_dim,), (right_dim,)), ((), ())), preferred_element_type=F32
    )


def head_lanes(head):
    return pl.ds(pl.multiple_of(head * HEAD_DIM, HEAD_DIM), HEAD_DIM)


def attend_head(quad):
    inv_root = 1.0 / math.sqrt(HEAD_DIM)
    q, k, v, g = (quad[:, n * HEAD_DIM : (n + 1) * HEAD_DIM] for n in range(4))
    scores = dot(q, k, 1, 1) * inv_root
    highest = jnp.max(scores, axis=1, keepdims=True)
    raised = jnp.exp(scores - highest)
    totals = jnp.sum(raised, axis=1, keepdims=True)
    attended = (dot(raised.astype(BF16), v) / totals).astype(BF16)
    weights = (raised * (1.0 / totals)).astype(BF16)
    inner = jnp.sum(g.astype(F32) * attended.astype(F32), axis=1, keepdims=True)
    grad_scores = dot(g, v, 1, 1)
    grad_logits = (weights.astype(F32) * (grad_scores - inner) * inv_root).astype(BF16)
    grad_q = dot(grad_logits, k).astype(BF16)
    grad_k = dot(grad_logits, q, 0, 0).astype(BF16)
    grad_v = dot(weights, g, 0, 0).astype(BF16)
    return jnp.concatenate([attended, grad_q, grad_k, grad_v], axis=1)


def pick_matrix(masks, kept):
    rows, tokens = masks[0].shape
    upto = (
        lax.broadcasted_iota(jnp.int32, (tokens, tokens), 0)
        <= lax.broadcasted_iota(jnp.int32, (tokens, tokens), 1)
    ).astype(BF16)
    slot = lax.broadcasted_iota(jnp.int32, (kept, tokens), 0).astype(F32)
    before = jnp.zeros((1, 1), F32)
    picks = []
    for mask in masks:
        rank = dot(mask, upto)[0:1]
        place = jnp.where(mask[0:1].astype(F32) > 0.5, rank + (before - 1.0), -1.0)
        picks.append((slot == place).astype(F32).astype(BF16))
        before = before + rank[:, tokens - 1 : tokens]
    return jnp.concatenate(picks, axis=1)


def gather_rows(pick, blocks):
    return dot(pick, jnp.concatenate(blocks, axis=0)).astype(BF16)


def pack_body(plan, q_ref, k_ref, v_ref, g_ref, mask_ref, *out_refs):
    win_count, per, extra, tokens = plan
    me = lax.axis_index("win")
    mask = jnp.broadcast_to(mask_ref[...].astype(F32), (MASK_ROWS, tokens)).astype(BF16)
    refs = (q_ref, k_ref, v_ref, g_ref)
    for step in range(1, win_count):
        out = out_refs[step - 1]
        for one in range(per):
            lanes = head_lanes((me ^ step) * per + one)
            for n, ref in enumerate(refs):
                at = one * QUAD + n * HEAD_DIM
                out[0:tokens, at : at + HEAD_DIM] = ref[0, :, lanes]
        out[tokens : tokens + MASK_ROWS, :] = jnp.zeros((MASK_ROWS, per * QUAD), BF16)
        out[tokens : tokens + MASK_ROWS, 0:tokens] = mask
    if extra:
        out = out_refs[win_count - 1]
        for one in range(extra):
            head = win_count * per + one
            for n, ref in enumerate(refs):
                at = one * QUAD + n * HEAD_DIM
                out[:, at : at + HEAD_DIM] = ref[0, :, head * HEAD_DIM : (head + 1) * HEAD_DIM]


def main_body(plan, q_ref, k_ref, v_ref, g_ref, mask_ref, *refs):
    win_count, per, extra, tokens = plan
    kept = win_count * tokens // 2
    got, outs, masks_out = refs[: win_count - 1], refs[win_count - 1 : -1], refs[-1]
    me = lax.axis_index("win")
    masks = [jnp.broadcast_to(mask_ref[...].astype(F32), (MASK_ROWS, tokens)).astype(BF16)]
    masks += [ref[tokens : tokens + MASK_ROWS, 0:tokens] for ref in got]
    for n, mask in enumerate(masks):
        masks_out[n] = mask
    pick = pick_matrix(masks, kept)
    for one in range(per):
        lanes = head_lanes(me * per + one)
        mine = jnp.concatenate([ref[0, :, lanes] for ref in (q_ref, k_ref, v_ref, g_ref)], axis=1)
        at = slice(one * QUAD, (one + 1) * QUAD)
        result = attend_head(gather_rows(pick, [mine] + [ref[0:tokens, at] for ref in got]))
        for n, out in enumerate(outs):
            out[:, at] = dot(pick[:, n * tokens : (n + 1) * tokens], result, 0, 0).astype(BF16)


def extra_body(plan, masks_ref, *refs):
    win_count, per, extra, tokens = plan
    kept = win_count * tokens // 2
    blocks, out = refs[:-1], refs[-1]
    pick = pick_matrix([masks_ref[n] for n in range(win_count)], kept)
    for one in range(extra):
        at = slice(one * QUAD, (one + 1) * QUAD)
        result = attend_head(gather_rows(pick, [ref[:, at] for ref in blocks]))
        out[:, at] = dot(pick[:, 0:tokens], result, 0, 0).astype(BF16)


def place_body(plan, *refs):
    win_count, per, extra, tokens = plan
    backs, outs = refs[:-4], refs[-4:]
    me = lax.axis_index("win")
    for step in range(win_count):
        for one in range(per):
            lanes = head_lanes((me ^ step) * per + one)
            for n, out in enumerate(outs):
                at = one * QUAD + n * HEAD_DIM
                out[0, :, lanes] = backs[step][:, at : at + HEAD_DIM]
    for one in range(extra):
        head = win_count * per + one
        for n, out in enumerate(outs):
            at = one * QUAD + n * HEAD_DIM
            out[0, :, head * HEAD_DIM : (head + 1) * HEAD_DIM] = backs[win_count][:, at : at + HEAD_DIM]


def exchange(array, step):
    count = lax.axis_size("win")
    return lax.ppermute(array, "win", [(n, n ^ step) for n in range(count)])


def shards_by_head(queries, key_vectors, value_vectors, out_grad, keep_mask):
    win_count = lax.axis_size("win")
    tokens, feat_dev = queries.shape[1:]
    head_count = feat_dev // HEAD_DIM
    per, extra = head_count // win_count, head_count % win_count
    plan = (win_count, per, extra, tokens)
    steps = range(1, win_count)
    arrays = (queries, key_vectors, value_vectors, out_grad)
    kept = win_count * tokens // 2
    cost = pl.CostEstimate(
        flops=2 * kept * kept * HEAD_DIM * 12, bytes_accessed=1 << 20, transcendentals=kept * kept
    )

    def call(body, out_shape, *operands):
        return pl.pallas_call(
            functools.partial(body, plan), out_shape=out_shape, cost_estimate=cost
        )(*operands)

    def shape(rows, heads):
        return jax.ShapeDtypeStruct((rows, heads * QUAD), BF16)

    packed = call(
        pack_body,
        [shape(tokens + MASK_ROWS, per)] * (win_count - 1) + [shape(tokens, extra)] * bool(extra),
        *arrays,
        keep_mask,
    )
    got = {step: exchange(packed[step - 1], step) for step in reversed(steps)}
    blocks = {0: packed[-1]}
    if extra:
        span = win_count // 2
        while span:
            for have in sorted(blocks):
                blocks[have ^ span] = exchange(blocks[have], span)
            span //= 2
    *results, masks = call(
        main_body,
        [shape(tokens, per)] * win_count
        + [jax.ShapeDtypeStruct((win_count, MASK_ROWS, tokens), BF16)],
        *arrays,
        keep_mask,
        *[got[step] for step in steps],
    )
    backs = [results[0]] + [exchange(results[step], step) for step in steps]
    if extra:
        backs.append(
            call(extra_body, shape(tokens, extra), masks, *[blocks[n] for n in range(win_count)])
        )
    return call(
        place_body, [jax.ShapeDtypeStruct(queries.shape, BF16)] * 4, *backs
    )


def fold_blocks(step_fn, carried, arrays):
    count = arrays[0].shape[0]
    width = 512 if count % 512 == 0 else count
    blocks = tuple(
        (member.reshape((count // width, width) + member.shape[1:]) for member in arrays)
    )

    def inner_step(state, current):
        return (step_fn(state, current), None)

    result, unused = lax.scan(inner_step, carried, blocks)
    return result


def shards(queries, key_vectors, value_vectors, out_grad, keep_mask):
    win_count = lax.axis_size("win")
    win_index = lax.axis_index("win")
    tok_rows = queries.shape[1]
    feat_dev = queries.shape[2]
    head_count = feat_dev // HEAD_DIM
    slot_rows = tok_rows // win_count
    own_rows = tok_rows // 2
    inv_root = 1.0 / math.sqrt(HEAD_DIM)
    kept_flag = keep_mask[0]
    kept_here = jnp.sum(kept_flag)
    counts = lax.all_gather(kept_here.reshape(1), "win", axis=0, tiled=True)
    starts = jnp.cumsum(counts) - counts
    ends = starts + counts
    start_here = starts[win_index]
    kept_order = jnp.argsort(1 - kept_flag, stable=True)
    kept_rank = jnp.cumsum(kept_flag) - 1
    slot_index = jnp.arange(tok_rows, dtype=jnp.int32)
    target = slot_index // slot_rows
    within = slot_index % slot_rows
    leading = start_here + jnp.mod(target - start_here, win_count)
    global_pos = leading + within * win_count
    send_live = global_pos < start_here + kept_here
    send_rows = kept_order[jnp.clip(global_pos - start_here, 0, tok_rows - 1)]

    def pack(matrix):
        return jnp.where(send_live[:, None], matrix[0][send_rows], jnp.zeros((), matrix.dtype))

    own_index = jnp.arange(own_rows, dtype=jnp.int32)
    wanted = own_index * win_count + win_index
    source = jnp.sum((ends[None, :] <= wanted[:, None]).astype(jnp.int32), axis=1)
    source_start = starts[source]
    source_lead = source_start + jnp.mod(win_index - source_start, win_count)
    recv_rows = source * slot_rows + (wanted - source_lead) // win_count

    def unpack(matrix):
        return matrix[recv_rows]

    back_start = starts[target]
    back_lead = back_start + jnp.mod(win_index - back_start, win_count)
    back_global = back_lead + within * win_count
    back_live = back_global < ends[target]
    back_rows = jnp.clip(back_global // win_count, 0, own_rows - 1)

    def repack(matrix):
        return jnp.where(back_live[:, None], matrix[back_rows], jnp.zeros((), matrix.dtype))

    global_here = start_here + kept_rank
    owner = jnp.mod(global_here, win_count)
    owner_lead = start_here + jnp.mod(owner - start_here, win_count)
    land_rows = jnp.clip(
        owner * slot_rows + (global_here - owner_lead) // win_count, 0, tok_rows - 1
    )

    def place(matrix):
        return jnp.where(kept_flag[:, None] == 1, matrix[land_rows], jnp.zeros((), matrix.dtype))[
            None
        ]

    def heads_view(matrix):
        return matrix.reshape(matrix.shape[0], head_count, HEAD_DIM)

    got_query, got_key, got_value = (
        lax.all_to_all(pack(queries), "win", split_axis=0, concat_axis=0, tiled=True),
        lax.all_to_all(pack(key_vectors), "win", split_axis=0, concat_axis=0, tiled=True),
        lax.all_to_all(pack(value_vectors), "win", split_axis=0, concat_axis=0, tiled=True),
    )
    query_rows = unpack(got_query)
    key_rows = unpack(got_key)
    value_rows = unpack(got_value)
    query_heads = heads_view(query_rows)

    def soft_step(carried, current):
        highest, totals, summed = carried
        block_keys, block_values = current
        scores = (
            jnp.einsum(
                "qhe,khe->hqk",
                query_heads,
                heads_view(block_keys),
                preferred_element_type=jnp.float32,
            )
            * inv_root
        )
        peak_new = jnp.maximum(highest, jnp.max(scores, axis=-1))
        shrink = jnp.exp(highest - peak_new)
        raised = jnp.exp(scores - peak_new[..., None])
        totals = totals * shrink + jnp.sum(raised, axis=-1)
        summed = summed * shrink.T[..., None] + jnp.einsum(
            "hqk,khe->qhe",
            raised.astype(jnp.bfloat16),
            heads_view(block_values),
            preferred_element_type=jnp.float32,
        )
        return (peak_new, totals, summed)

    start_state = (
        jnp.full((head_count, own_rows), -jnp.inf, jnp.float32),
        jnp.zeros((head_count, own_rows), jnp.float32),
        jnp.zeros((own_rows, head_count, HEAD_DIM), jnp.float32),
    )
    highest, totals, summed = fold_blocks(
        soft_step,
        start_state,
        (
            lax.all_gather(key_rows, "win", axis=0, tiled=True),
            lax.all_gather(value_rows, "win", axis=0, tiled=True),
        ),
    )
    log_total = highest + jnp.log(totals)
    attended = (summed / totals.T[..., None]).astype(jnp.bfloat16)
    grad_rows = unpack(
        lax.all_to_all(pack(out_grad), "win", split_axis=0, concat_axis=0, tiled=True)
    )
    grad_heads = heads_view(grad_rows)
    inner = jnp.sum(grad_heads.astype(jnp.float32) * attended.astype(jnp.float32), axis=-1).T

    def query_step(carried, current):
        block_keys, block_values = current
        key_heads = heads_view(block_keys)
        scores = (
            jnp.einsum("qhe,khe->hqk", query_heads, key_heads, preferred_element_type=jnp.float32)
            * inv_root
        )
        weights = jnp.exp(scores - log_total[..., None]).astype(jnp.bfloat16)
        grad_scores = jnp.einsum(
            "qhe,khe->hqk", grad_heads, heads_view(block_values), preferred_element_type=jnp.float32
        )
        grad_logits = (
            weights.astype(jnp.float32) * (grad_scores - inner[..., None]) * inv_root
        ).astype(jnp.bfloat16)
        return carried + jnp.einsum(
            "hqk,khe->qhe", grad_logits, key_heads, preferred_element_type=jnp.float32
        )

    query_zero = jnp.zeros((own_rows, head_count, HEAD_DIM), jnp.float32)
    grad_query = fold_blocks(
        query_step,
        query_zero,
        (
            lax.all_gather(key_rows, "win", axis=0, tiled=True),
            lax.all_gather(value_rows, "win", axis=0, tiled=True),
        ),
    )
    all_log, all_inner = (
        lax.all_gather(log_total.T, "win", axis=0, tiled=True),
        lax.all_gather(inner.T, "win", axis=0, tiled=True),
    )
    own_key_heads = heads_view(key_rows)
    own_value_heads = heads_view(value_rows)

    def key_step(carried, current):
        key_total, value_total = carried
        block_queries, block_grads, block_log, block_inner = current
        query_block = heads_view(block_queries)
        grad_block = heads_view(block_grads)
        scores = (
            jnp.einsum(
                "khe,qhe->hkq", own_key_heads, query_block, preferred_element_type=jnp.float32
            )
            * inv_root
        )
        weights = jnp.exp(scores - block_log.T[:, None, :]).astype(jnp.bfloat16)
        value_total = value_total + jnp.einsum(
            "hkq,qhe->khe", weights, grad_block, preferred_element_type=jnp.float32
        )
        grad_scores = jnp.einsum(
            "khe,qhe->hkq", own_value_heads, grad_block, preferred_element_type=jnp.float32
        )
        grad_logits = (
            weights.astype(jnp.float32) * (grad_scores - block_inner.T[:, None, :]) * inv_root
        ).astype(jnp.bfloat16)
        key_total = key_total + jnp.einsum(
            "hkq,qhe->khe", grad_logits, query_block, preferred_element_type=jnp.float32
        )
        return (key_total, value_total)

    key_rows_count = key_rows.shape[0]
    empty_grads = jnp.zeros((key_rows_count, head_count, HEAD_DIM), jnp.float32)
    key_total, value_total = fold_blocks(
        key_step,
        (empty_grads, empty_grads),
        (
            lax.all_gather(query_rows, "win", axis=0, tiled=True),
            lax.all_gather(grad_rows, "win", axis=0, tiled=True),
            all_log,
            all_inner,
        ),
    )
    grad_key = key_total.reshape(key_rows_count, feat_dev).astype(jnp.bfloat16)
    grad_value = value_total.reshape(key_rows_count, feat_dev).astype(jnp.bfloat16)
    attended_flat = attended.reshape(own_rows, feat_dev)
    grad_query_flat = grad_query.reshape(own_rows, feat_dev).astype(jnp.bfloat16)
    back_attended, back_query, back_key, back_value = (
        lax.all_to_all(repack(attended_flat), "win", split_axis=0, concat_axis=0, tiled=True),
        lax.all_to_all(repack(grad_query_flat), "win", split_axis=0, concat_axis=0, tiled=True),
        lax.all_to_all(repack(grad_key), "win", split_axis=0, concat_axis=0, tiled=True),
        lax.all_to_all(repack(grad_value), "win", split_axis=0, concat_axis=0, tiled=True),
    )
    grad_key_out = place(back_key)
    grad_value_out = place(back_value)
    return (place(back_attended), place(back_query), grad_key_out, grad_value_out)


def by_plan(queries, key_vectors, value_vectors, out_grad, keep_mask):
    win_count = lax.axis_size("win")
    enough = queries.shape[2] // HEAD_DIM >= win_count
    paired = win_count > 1 and win_count & (win_count - 1) == 0
    shaped = queries.shape[1] % 16 == 0 and queries.shape[1] == HEAD_DIM
    run = shards_by_head if enough and paired and shaped else shards
    return run(queries, key_vectors, value_vectors, out_grad, keep_mask)


def solution(mesh):
    placed = (
        P(("groups", "samp"), "win", "head"),
        P(("groups", "samp"), "win", "head"),
        P(("groups", "samp"), "win", "head"),
        P(("groups", "samp"), "win", "head"),
        P(("groups", "samp"), "win"),
    )
    return jax.shard_map(
        by_plan,
        mesh=mesh,
        in_specs=placed,
        out_specs=(
            P(("groups", "samp"), "win", "head"),
            P(("groups", "samp"), "win", "head"),
            P(("groups", "samp"), "win", "head"),
            P(("groups", "samp"), "win", "head"),
        ),
        check_vma=False,
    )
```

```python
import functools
import math

import jax
import jax.numpy as jnp
from jax import lax
from jax.experimental import pallas as pl
from jax.experimental.pallas import tpu as pltpu
from jax.sharding import PartitionSpec as P

HEAD_DIM = 128
MASK_ROWS = 16
VMEM_BYTES = 16 << 20
QUAD = 4 * HEAD_DIM
BF16 = jnp.bfloat16
F32 = jnp.float32


def dot(left, right, left_dim=1, right_dim=0):
    return lax.dot_general(
        left, right, (((left_dim,), (right_dim,)), ((), ())), preferred_element_type=F32
    )


def head_lanes(head):
    if isinstance(head, int):
        return pl.ds(head * HEAD_DIM, HEAD_DIM)
    return pl.ds(pl.multiple_of(head * HEAD_DIM, HEAD_DIM), HEAD_DIM)


def attend_head(quad):
    inv_root = 1.0 / math.sqrt(HEAD_DIM)
    q, k, v, g = (quad[:, n * HEAD_DIM : (n + 1) * HEAD_DIM] for n in range(4))
    scores = dot(q, k, 1, 1) * inv_root
    highest = jnp.max(scores, axis=1, keepdims=True)
    raised = jnp.exp(scores - highest)
    totals = jnp.sum(raised, axis=1, keepdims=True)
    attended = (dot(raised.astype(BF16), v) / totals).astype(BF16)
    weights = (raised * (1.0 / totals)).astype(BF16)
    inner = jnp.sum(g.astype(F32) * attended.astype(F32), axis=1, keepdims=True)
    grad_scores = dot(g, v, 1, 1)
    grad_logits = (weights.astype(F32) * (grad_scores - inner) * inv_root).astype(BF16)
    grad_q = dot(grad_logits, k).astype(BF16)
    grad_k = dot(grad_logits, q, 0, 0).astype(BF16)
    grad_v = dot(weights, g, 0, 0).astype(BF16)
    return jnp.concatenate([attended, grad_q, grad_k, grad_v], axis=1)


def pick_matrix(masks, kept):
    rows, tokens = masks[0].shape
    upto = (
        lax.broadcasted_iota(jnp.int32, (tokens, tokens), 0)
        <= lax.broadcasted_iota(jnp.int32, (tokens, tokens), 1)
    ).astype(BF16)
    slot = lax.broadcasted_iota(jnp.int32, (kept, tokens), 0).astype(F32)
    before = jnp.zeros((1, 1), F32)
    picks = []
    for mask in masks:
        rank = dot(mask, upto)[0:1]
        place = jnp.where(mask[0:1].astype(F32) > 0.5, rank + (before - 1.0), -1.0)
        picks.append((slot == place).astype(F32).astype(BF16))
        before = before + rank[:, tokens - 1 : tokens]
    return jnp.concatenate(picks, axis=1)


def pieces(plan, step):
    order, per, extra, tokens = plan
    win_count = len(order)
    shared = extra if step == len(order) // 2 else 0
    return 4 * tokens * per, 4 * tokens * shared


def pack_body(plan, q_ref, k_ref, v_ref, g_ref, mask_ref, *refs):
    order, per, extra, tokens = plan
    win_count = len(order)
    outs, (mask_here, sems) = refs[:-2], refs[-2:]
    me = lax.axis_index("win")
    copies = [pltpu.make_async_copy(mask_ref, mask_here, sems.at[0])]

    def lay(out, at, head):
        for n, ref in enumerate((q_ref, k_ref, v_ref, g_ref)):
            copies.append(
                pltpu.make_async_copy(
                    ref.at[0, :, head_lanes(head)],
                    out.at[at + n * tokens : at + (n + 1) * tokens, :],
                    sems.at[len(copies)],
                )
            )

    for out, step in zip(outs, order):
        own, shared = pieces(plan, step)
        for one in range(per):
            lay(out, 4 * tokens * one, (me ^ step) * per + one)
        for one in range(extra if shared else 0):
            lay(out, own + MASK_ROWS + 4 * tokens * one, win_count * per + one)
    for one in range(extra):
        lay(outs[win_count], 4 * tokens * one, win_count * per + one)
    for copy in copies:
        copy.start()
    copies[0].wait()
    mask = jnp.broadcast_to(mask_here[...].astype(F32), (MASK_ROWS, tokens)).astype(BF16)
    own, _ = pieces(plan, 0)
    for out in outs[:win_count]:
        out[own : own + MASK_ROWS, :] = mask
    for copy in copies[1:]:
        copy.wait()


def quads(refs, at, tokens):
    return jnp.concatenate(
        [
            jnp.concatenate(
                [ref[start + n * tokens : start + (n + 1) * tokens, :] for n in range(4)], axis=1
            )
            for ref, start in zip(refs, at)
        ],
        axis=0,
    )


def put_back(out, at, pick, result, tokens):
    rows = dot(pick, result, 0, 0).astype(BF16)
    for n in range(4):
        out[at + n * tokens : at + (n + 1) * tokens, :] = rows[:, n * HEAD_DIM : (n + 1) * HEAD_DIM]


def main_body(plan, *refs):
    order, per, extra, tokens = plan
    win_count = len(order)
    kept = win_count * tokens // 2
    got, outs, masks_out = refs[:win_count], refs[win_count:-1], refs[-1]
    own, _ = pieces(plan, 0)
    masks = [ref[own : own + MASK_ROWS, :] for ref in got]
    for n, mask in enumerate(masks):
        masks_out[n] = mask
    pick = pick_matrix(masks, kept)
    for one in range(per):
        at = 4 * tokens * one
        rows = dot(pick, quads(got, [at] * win_count, tokens)).astype(BF16)
        result = attend_head(rows)
        for n, out in enumerate(outs):
            put_back(out, at, pick[:, n * tokens : (n + 1) * tokens], result, tokens)


def extra_body(plan, masks_ref, *refs):
    order, per, extra, tokens = plan
    win_count = len(order)
    kept = win_count * tokens // 2
    blocks, out = refs[:-1], refs[-1]
    pick = pick_matrix([masks_ref[n] for n in range(win_count)], kept)
    own, _ = pieces(plan, 0)
    for one in range(extra):
        at = 4 * tokens * one
        starts = [at + (own + MASK_ROWS if pieces(plan, step)[1] else 0) for step in order]
        rows = dot(pick, quads(blocks, starts, tokens)).astype(BF16)
        put_back(out, at, pick[:, 0:tokens], attend_head(rows), tokens)


def place_body(plan, *refs):
    order, per, extra, tokens = plan
    win_count = len(order)
    backs, outs, sems = refs[:-5], refs[-5:-1], refs[-1]
    me = lax.axis_index("win")
    made = [
        (back, one, head_lanes((me ^ step) * per + one))
        for back, step in zip(backs, order)
        for one in range(per)
    ]
    made += [(backs[win_count], one, head_lanes(win_count * per + one)) for one in range(extra)]
    copies = []
    for back, one, lanes in made:
        for n, out in enumerate(outs):
            at = (4 * one + n) * tokens
            copies.append(
                pltpu.make_async_copy(
                    back.at[at : at + tokens, :], out.at[0, :, lanes], sems.at[len(copies)]
                )
            )
    for copy in copies:
        copy.start()
    for copy in copies:
        copy.wait()


def exchange(array, step):
    if step == 0:
        return array
    count = lax.axis_size("win")
    return lax.ppermute(array, "win", [(n, n ^ step) for n in range(count)])


def after(array, other):
    return lax.optimization_barrier((array, other))


def shards_by_head(queries, key_vectors, value_vectors, out_grad, keep_mask):
    win_count = lax.axis_size("win")
    tokens, feat_dev = queries.shape[1:]
    head_count = feat_dev // HEAD_DIM
    per, extra = head_count // win_count, head_count % win_count
    order = [0,2,1,3]
    plan = (order, per, extra, tokens)
    arrays = (queries, key_vectors, value_vectors, out_grad)
    kept = win_count * tokens // 2
    cost = pl.CostEstimate(
        flops=2 * kept * kept * HEAD_DIM * 12, bytes_accessed=1 << 20, transcendentals=kept * kept
    )
    in_hbm = pl.BlockSpec(memory_space=pltpu.HBM)

    def call(body, out_shape, *operands, **specs):
        return pl.pallas_call(
            functools.partial(body, plan),
            out_shape=out_shape,
            cost_estimate=cost,
            compiler_params=pltpu.CompilerParams(vmem_limit_bytes=VMEM_BYTES),
            **specs,
        )(*operands)

    def shape(rows):
        return jax.ShapeDtypeStruct((rows, HEAD_DIM), BF16)

    sent = [sum(pieces(plan, step)) + MASK_ROWS for step in order]
    shared = sum(bool(pieces(plan, step)[1]) for step in order)
    packed = call(
        pack_body,
        [shape(rows) for rows in sent] + [shape(4 * tokens * extra)] * bool(extra),
        *[pltpu.with_memory_space_constraint(one, pltpu.HBM) for one in (*arrays, keep_mask)],
        in_specs=[in_hbm] * 5,
        scratch_shapes=[
            pltpu.VMEM(keep_mask.shape, keep_mask.dtype),
            pltpu.SemaphoreType.DMA((1 + 4 * (head_count + extra * shared),)),
        ],
    )
    got = {step: exchange(out, step) for step, out in zip(order, packed)}
    if extra:
        blocks = {0: packed[win_count]}
        blocks.update({step: got[step] for step in order if pieces(plan, step)[1]})
        for step in range(1, win_count):
            if step not in blocks:
                low = step & -step
                near = blocks[step ^ low]
                blocks[step] = exchange(near[near.shape[0] - 4 * tokens * extra :], low)
    *results, masks = call(
        main_body,
        [shape(4 * tokens * per)] * win_count
        + [jax.ShapeDtypeStruct((win_count, MASK_ROWS, tokens), BF16)],
        *[got[step] for step in order],
    )
    backs = [exchange(result, step) for step, result in zip(order, results)]
    if extra:
        backs.append(
            call(
                extra_body,
                shape(4 * tokens * extra),
                masks,
                *[blocks[step] for step in order],
            )
        )
    return call(
        place_body,
        [jax.ShapeDtypeStruct(queries.shape, BF16)] * 4,
        *backs,
        out_specs=[in_hbm] * 4,
        scratch_shapes=[pltpu.SemaphoreType.DMA((4 * head_count,))],
    )


def fold_blocks(step_fn, carried, arrays):
    count = arrays[0].shape[0]
    width = 512 if count % 512 == 0 else count
    blocks = tuple(
        (member.reshape((count // width, width) + member.shape[1:]) for member in arrays)
    )

    def inner_step(state, current):
        return (step_fn(state, current), None)

    result, unused = lax.scan(inner_step, carried, blocks)
    return result


def shards(queries, key_vectors, value_vectors, out_grad, keep_mask):
    win_count = lax.axis_size("win")
    win_index = lax.axis_index("win")
    tok_rows = queries.shape[1]
    feat_dev = queries.shape[2]
    head_count = feat_dev // HEAD_DIM
    slot_rows = tok_rows // win_count
    own_rows = tok_rows // 2
    inv_root = 1.0 / math.sqrt(HEAD_DIM)
    kept_flag = keep_mask[0]
    kept_here = jnp.sum(kept_flag)
    counts = lax.all_gather(kept_here.reshape(1), "win", axis=0, tiled=True)
    starts = jnp.cumsum(counts) - counts
    ends = starts + counts
    start_here = starts[win_index]
    kept_order = jnp.argsort(1 - kept_flag, stable=True)
    kept_rank = jnp.cumsum(kept_flag) - 1
    slot_index = jnp.arange(tok_rows, dtype=jnp.int32)
    target = slot_index // slot_rows
    within = slot_index % slot_rows
    leading = start_here + jnp.mod(target - start_here, win_count)
    global_pos = leading + within * win_count
    send_live = global_pos < start_here + kept_here
    send_rows = kept_order[jnp.clip(global_pos - start_here, 0, tok_rows - 1)]

    def pack(matrix):
        return jnp.where(send_live[:, None], matrix[0][send_rows], jnp.zeros((), matrix.dtype))

    own_index = jnp.arange(own_rows, dtype=jnp.int32)
    wanted = own_index * win_count + win_index
    source = jnp.sum((ends[None, :] <= wanted[:, None]).astype(jnp.int32), axis=1)
    source_start = starts[source]
    source_lead = source_start + jnp.mod(win_index - source_start, win_count)
    recv_rows = source * slot_rows + (wanted - source_lead) // win_count

    def unpack(matrix):
        return matrix[recv_rows]

    back_start = starts[target]
    back_lead = back_start + jnp.mod(win_index - back_start, win_count)
    back_global = back_lead + within * win_count
    back_live = back_global < ends[target]
    back_rows = jnp.clip(back_global // win_count, 0, own_rows - 1)

    def repack(matrix):
        return jnp.where(back_live[:, None], matrix[back_rows], jnp.zeros((), matrix.dtype))

    global_here = start_here + kept_rank
    owner = jnp.mod(global_here, win_count)
    owner_lead = start_here + jnp.mod(owner - start_here, win_count)
    land_rows = jnp.clip(
        owner * slot_rows + (global_here - owner_lead) // win_count, 0, tok_rows - 1
    )

    def place(matrix):
        return jnp.where(kept_flag[:, None] == 1, matrix[land_rows], jnp.zeros((), matrix.dtype))[
            None
        ]

    def heads_view(matrix):
        return matrix.reshape(matrix.shape[0], head_count, HEAD_DIM)

    got_query, got_key, got_value = (
        lax.all_to_all(pack(queries), "win", split_axis=0, concat_axis=0, tiled=True),
        lax.all_to_all(pack(key_vectors), "win", split_axis=0, concat_axis=0, tiled=True),
        lax.all_to_all(pack(value_vectors), "win", split_axis=0, concat_axis=0, tiled=True),
    )
    query_rows = unpack(got_query)
    key_rows = unpack(got_key)
    value_rows = unpack(got_value)
    query_heads = heads_view(query_rows)

    def soft_step(carried, current):
        highest, totals, summed = carried
        block_keys, block_values = current
        scores = (
            jnp.einsum(
                "qhe,khe->hqk",
                query_heads,
                heads_view(block_keys),
                preferred_element_type=jnp.float32,
            )
            * inv_root
        )
        peak_new = jnp.maximum(highest, jnp.max(scores, axis=-1))
        shrink = jnp.exp(highest - peak_new)
        raised = jnp.exp(scores - peak_new[..., None])
        totals = totals * shrink + jnp.sum(raised, axis=-1)
        summed = summed * shrink.T[..., None] + jnp.einsum(
            "hqk,khe->qhe",
            raised.astype(jnp.bfloat16),
            heads_view(block_values),
            preferred_element_type=jnp.float32,
        )
        return (peak_new, totals, summed)

    start_state = (
        jnp.full((head_count, own_rows), -jnp.inf, jnp.float32),
        jnp.zeros((head_count, own_rows), jnp.float32),
        jnp.zeros((own_rows, head_count, HEAD_DIM), jnp.float32),
    )
    highest, totals, summed = fold_blocks(
        soft_step,
        start_state,
        (
            lax.all_gather(key_rows, "win", axis=0, tiled=True),
            lax.all_gather(value_rows, "win", axis=0, tiled=True),
        ),
    )
    log_total = highest + jnp.log(totals)
    attended = (summed / totals.T[..., None]).astype(jnp.bfloat16)
    grad_rows = unpack(
        lax.all_to_all(pack(out_grad), "win", split_axis=0, concat_axis=0, tiled=True)
    )
    grad_heads = heads_view(grad_rows)
    inner = jnp.sum(grad_heads.astype(jnp.float32) * attended.astype(jnp.float32), axis=-1).T

    def query_step(carried, current):
        block_keys, block_values = current
        key_heads = heads_view(block_keys)
        scores = (
            jnp.einsum("qhe,khe->hqk", query_heads, key_heads, preferred_element_type=jnp.float32)
            * inv_root
        )
        weights = jnp.exp(scores - log_total[..., None]).astype(jnp.bfloat16)
        grad_scores = jnp.einsum(
            "qhe,khe->hqk", grad_heads, heads_view(block_values), preferred_element_type=jnp.float32
        )
        grad_logits = (
            weights.astype(jnp.float32) * (grad_scores - inner[..., None]) * inv_root
        ).astype(jnp.bfloat16)
        return carried + jnp.einsum(
            "hqk,khe->qhe", grad_logits, key_heads, preferred_element_type=jnp.float32
        )

    query_zero = jnp.zeros((own_rows, head_count, HEAD_DIM), jnp.float32)
    grad_query = fold_blocks(
        query_step,
        query_zero,
        (
            lax.all_gather(key_rows, "win", axis=0, tiled=True),
            lax.all_gather(value_rows, "win", axis=0, tiled=True),
        ),
    )
    all_log, all_inner = (
        lax.all_gather(log_total.T, "win", axis=0, tiled=True),
        lax.all_gather(inner.T, "win", axis=0, tiled=True),
    )
    own_key_heads = heads_view(key_rows)
    own_value_heads = heads_view(value_rows)

    def key_step(carried, current):
        key_total, value_total = carried
        block_queries, block_grads, block_log, block_inner = current
        query_block = heads_view(block_queries)
        grad_block = heads_view(block_grads)
        scores = (
            jnp.einsum(
                "khe,qhe->hkq", own_key_heads, query_block, preferred_element_type=jnp.float32
            )
            * inv_root
        )
        weights = jnp.exp(scores - block_log.T[:, None, :]).astype(jnp.bfloat16)
        value_total = value_total + jnp.einsum(
            "hkq,qhe->khe", weights, grad_block, preferred_element_type=jnp.float32
        )
        grad_scores = jnp.einsum(
            "khe,qhe->hkq", own_value_heads, grad_block, preferred_element_type=jnp.float32
        )
        grad_logits = (
            weights.astype(jnp.float32) * (grad_scores - block_inner.T[:, None, :]) * inv_root
        ).astype(jnp.bfloat16)
        key_total = key_total + jnp.einsum(
            "hkq,qhe->khe", grad_logits, query_block, preferred_element_type=jnp.float32
        )
        return (key_total, value_total)

    key_rows_count = key_rows.shape[0]
    empty_grads = jnp.zeros((key_rows_count, head_count, HEAD_DIM), jnp.float32)
    key_total, value_total = fold_blocks(
        key_step,
        (empty_grads, empty_grads),
        (
            lax.all_gather(query_rows, "win", axis=0, tiled=True),
            lax.all_gather(grad_rows, "win", axis=0, tiled=True),
            all_log,
            all_inner,
        ),
    )
    grad_key = key_total.reshape(key_rows_count, feat_dev).astype(jnp.bfloat16)
    grad_value = value_total.reshape(key_rows_count, feat_dev).astype(jnp.bfloat16)
    attended_flat = attended.reshape(own_rows, feat_dev)
    grad_query_flat = grad_query.reshape(own_rows, feat_dev).astype(jnp.bfloat16)
    back_attended, back_query, back_key, back_value = (
        lax.all_to_all(repack(attended_flat), "win", split_axis=0, concat_axis=0, tiled=True),
        lax.all_to_all(repack(grad_query_flat), "win", split_axis=0, concat_axis=0, tiled=True),
        lax.all_to_all(repack(grad_key), "win", split_axis=0, concat_axis=0, tiled=True),
        lax.all_to_all(repack(grad_value), "win", split_axis=0, concat_axis=0, tiled=True),
    )
    grad_key_out = place(back_key)
    grad_value_out = place(back_value)
    return (place(back_attended), place(back_query), grad_key_out, grad_value_out)


def by_plan(queries, key_vectors, value_vectors, out_grad, keep_mask):
    win_count = lax.axis_size("win")
    enough = queries.shape[2] // HEAD_DIM >= win_count
    paired = win_count > 1 and win_count & (win_count - 1) == 0
    shaped = queries.shape[1] % 16 == 0 and queries.shape[1] == HEAD_DIM
    run = shards_by_head if enough and paired and shaped else shards
    return run(queries, key_vectors, value_vectors, out_grad, keep_mask)


def solution(mesh):
    placed = (
        P(("groups", "samp"), "win", "head"),
        P(("groups", "samp"), "win", "head"),
        P(("groups", "samp"), "win", "head"),
        P(("groups", "samp"), "win", "head"),
        P(("groups", "samp"), "win"),
    )
    return jax.shard_map(
        by_plan,
        mesh=mesh,
        in_specs=placed,
        out_specs=(
            P(("groups", "samp"), "win", "head"),
            P(("groups", "samp"), "win", "head"),
            P(("groups", "samp"), "win", "head"),
            P(("groups", "samp"), "win", "head"),
        ),
        check_vma=False,
    )
```

```python
import functools
import math

import jax
import jax.numpy as jnp
from jax import lax
from jax.experimental import pallas as pl
from jax.experimental.pallas import tpu as pltpu
from jax.sharding import PartitionSpec as P

HEAD_DIM = 128
TILE_ROWS = 16
WINDOWS = 4
DROPPED = 64.0
VMEM_BYTES = 16 << 20
BF16 = jnp.bfloat16
F32 = jnp.float32


def dot(left, right, left_dim=1, right_dim=0):
    return lax.dot_general(
        left, right, (((left_dim,), (right_dim,)), ((), ())), preferred_element_type=F32
    )


def attend_head(rows):
    inv_root = 1.0 / math.sqrt(HEAD_DIM)
    q, k, v, g = (rows[:, n * HEAD_DIM : (n + 1) * HEAD_DIM] for n in range(4))
    scores = dot(q, k, 1, 1) * inv_root
    highest = jnp.max(scores, axis=1, keepdims=True)
    raised = jnp.exp(scores - highest)
    totals = jnp.sum(raised, axis=1, keepdims=True)
    attended = (dot(raised.astype(BF16), v) / totals).astype(BF16)
    weights = (raised * (1.0 / totals)).astype(BF16)
    inner = jnp.sum(g.astype(F32) * attended.astype(F32), axis=1, keepdims=True)
    grad_scores = dot(g, v, 1, 1)
    grad_logits = (weights.astype(F32) * (grad_scores - inner) * inv_root).astype(BF16)
    grad_q = dot(grad_logits, k).astype(BF16)
    grad_k = dot(grad_logits, q, 0, 0).astype(BF16)
    grad_v = dot(weights, g, 0, 0).astype(BF16)
    return jnp.concatenate([attended, grad_q, grad_k, grad_v], axis=1)


def side_by_side(ref):
    tokens = ref.shape[0] // 4
    return jnp.concatenate([ref[n * tokens : (n + 1) * tokens, :] for n in range(4)], axis=1)


def picks_of(blocks, kept, before):
    tokens = blocks[0].shape[0] // 4
    lead = (lax.broadcasted_iota(jnp.int32, (TILE_ROWS, HEAD_DIM), 1) == 0).astype(BF16)
    upto = (
        lax.broadcasted_iota(jnp.int32, (tokens, tokens), 0)
        <= lax.broadcasted_iota(jnp.int32, (tokens, tokens), 1)
    ).astype(BF16)
    slot = lax.broadcasted_iota(jnp.int32, (kept, tokens), 0).astype(F32)
    picks = []
    for block in blocks:
        live = dot(lead, block[0:tokens, :], 1, 1) < 0.5 * DROPPED
        rank = dot(live.astype(F32).astype(BF16), upto)[0:1]
        place = jnp.where(live[0:1], rank + (before - 1.0), -1.0)
        picks.append((slot == place).astype(F32).astype(BF16))
        before = before + rank[:, tokens - 1 : tokens]
    return jnp.concatenate(picks, axis=1), before


def put_back(out, picked, result):
    tokens = picked.shape[0]
    rows = dot(picked, result).astype(BF16)
    for n in range(4):
        out[n * tokens : (n + 1) * tokens, :] = rows[:, n * HEAD_DIM : (n + 1) * HEAD_DIM]


def head_lanes(head):
    if isinstance(head, int):
        return pl.ds(head * HEAD_DIM, HEAD_DIM)
    return pl.ds(pl.multiple_of(head * HEAD_DIM, HEAD_DIM), HEAD_DIM)


def pack_body(steps, q_ref, k_ref, v_ref, g_ref, mask_ref, *refs):
    outs, (mask_here, sems) = refs[:-2], refs[-2:]
    tokens = mask_ref.shape[1]
    me = lax.axis_index("win")
    copies = [pltpu.make_async_copy(mask_ref, mask_here, sems.at[0])]
    for out, step in zip(outs, steps):
        lanes = head_lanes(WINDOWS if step is None else me ^ step)
        for n, ref in enumerate((q_ref, k_ref, v_ref, g_ref)):
            copies.append(
                pltpu.make_async_copy(
                    ref.at[0, :, lanes],
                    out.at[n * tokens : (n + 1) * tokens, :],
                    sems.at[len(copies)],
                )
            )
    for copy in copies:
        copy.start()
    copies[0].wait()
    live = jnp.broadcast_to(mask_here[...].astype(F32), (TILE_ROWS, tokens)).astype(BF16)
    share = jnp.full((TILE_ROWS, HEAD_DIM), 1.0 / TILE_ROWS, BF16)
    keep = dot(live, share, 0, 0)
    mark = (1.0 - keep) * DROPPED
    for copy in copies[1:]:
        copy.wait()
    for out, step in zip(outs, steps):
        if step is not None:
            out[0:tokens, :] = (out[0:tokens, :].astype(F32) * keep + mark).astype(BF16)


def turned(pick):
    kept = pick.shape[0]
    unit = (
        lax.broadcasted_iota(jnp.int32, (kept, kept), 0)
        == lax.broadcasted_iota(jnp.int32, (kept, kept), 1)
    ).astype(F32).astype(BF16)
    return dot(pick, unit, 0, 0).astype(BF16)


def early_body(own, near, far, pick_out, turned_out, rows_out, used_out):
    kept = pick_out.shape[0]
    blocks = (own, near, far)
    pick, used = picks_of(blocks, kept, jnp.zeros((1, 1), F32))
    pick_out[...] = pick
    used_out[...] = jnp.broadcast_to(used, used_out.shape)
    rows_out[...] = dot(pick, jnp.concatenate([side_by_side(ref) for ref in blocks], axis=0)).astype(
        BF16
    )
    turned_out[...] = turned(pick)


def main_body(cross, turned_ref, rows_ref, used_ref, own_out, near_out, far_out, cross_out, last_out):
    kept = rows_ref.shape[0]
    tokens = cross.shape[0] // 4
    last, _ = picks_of((cross,), kept, used_ref[0:1, 0:1])
    last_out[...] = last
    rows = rows_ref[...] + dot(last, side_by_side(cross)).astype(BF16)
    result = attend_head(rows)
    put_back(cross_out, turned(last), result)
    for n, out in ((1, near_out), (2, far_out), (0, own_out)):
        put_back(out, turned_ref[n * tokens : (n + 1) * tokens, :], result)


def shared_early_body(pick_ref, own, near, far, rows_out):
    blocks = (own, near, far)
    rows_out[...] = dot(
        pick_ref[...], jnp.concatenate([side_by_side(ref) for ref in blocks], axis=0)
    ).astype(BF16)


def placed(back, tokens, lanes, outs, sems):
    return [
        pltpu.make_async_copy(
            back.at[n * tokens : (n + 1) * tokens, :], out.at[0, :, lanes], sems.at[n]
        )
        for n, out in enumerate(outs)
    ]


def last_body(steps, *refs):
    backs = list(refs[: len(steps) + 1])
    relayed = backs.pop(3)
    relpick_ref, turned_ref, rows_ref = refs[len(steps) + 1 : -6]
    outs, shared, sems = refs[-6:-2], refs[-2], refs[-1]
    tokens = outs[0].shape[1]
    me = lax.axis_index("win")
    copies = []
    for n, (back, step) in enumerate(zip(backs, steps)):
        copies += placed(back, tokens, head_lanes(me ^ step), outs, sems.at[n])
    for copy in copies:
        copy.start()
    rows = rows_ref[...] + dot(relpick_ref[...], side_by_side(relayed)).astype(BF16)
    put_back(shared, turned_ref[0:tokens, :], attend_head(rows))
    more = placed(shared, tokens, head_lanes(WINDOWS), outs, sems.at[len(steps)])
    for copy in more:
        copy.start()
    for copy in copies + more:
        copy.wait()


def exchange(array, step):
    return lax.ppermute(array, "win", [(n, n ^ step) for n in range(WINDOWS)])


def after(array, other):
    return lax.optimization_barrier((array, other))


def shards_by_head(queries, key_vectors, value_vectors, out_grad, keep_mask):
    tokens = queries.shape[1]
    kept = WINDOWS * tokens // 2
    in_hbm = pl.BlockSpec(memory_space=pltpu.HBM)
    block = jax.ShapeDtypeStruct((4 * tokens, HEAD_DIM), BF16)
    rows = jax.ShapeDtypeStruct((kept, 4 * HEAD_DIM), BF16)
    turned_picks = jax.ShapeDtypeStruct((3 * tokens, kept), BF16)
    whole = jax.ShapeDtypeStruct(queries.shape, BF16)

    def picks(windows):
        return jax.ShapeDtypeStruct((kept, windows * tokens), BF16)

    def call(body, out_shape, *operands, flops=0, **specs):
        return pl.pallas_call(
            body,
            out_shape=out_shape,
            cost_estimate=pl.CostEstimate(flops=flops, bytes_accessed=0, transcendentals=0),
            compiler_params=pltpu.CompilerParams(vmem_limit_bytes=VMEM_BYTES),
            **specs,
        )(*operands)

    pinned = [
        pltpu.with_memory_space_constraint(one, pltpu.HBM)
        for one in (queries, key_vectors, value_vectors, out_grad, keep_mask)
    ]

    def pack(*steps):
        return call(
            functools.partial(pack_body, steps),
            [block] * len(steps),
            *pinned,
            in_specs=[in_hbm] * 5,
            scratch_shapes=[
                pltpu.VMEM(keep_mask.shape, keep_mask.dtype),
                pltpu.SemaphoreType.DMA((1 + 4 * len(steps),)),
            ],
        )

    (far,) = pack(2)
    cross, near, own, shared = pack(3, 1, 0, None)
    got_far = exchange(far, 2)
    got_cross = exchange(cross, 3)
    got_near = exchange(near, 1)
    late, got_far = after(shared, got_far)
    shared_far = exchange(late, 2)
    shared_near = exchange(late, 1)
    pick, turned_pick, some_rows, used = call(
        early_body,
        [picks(3), turned_picks, rows, jax.ShapeDtypeStruct((8, HEAD_DIM), F32)],
        own,
        got_near,
        got_far,
        flops=1 << 28,
    )
    own_result, near_result, far_result, cross_result, last = call(
        main_body, [block] * 4 + [picks(1)], got_cross, turned_pick, some_rows, used, flops=1 << 29
    )
    back_far = exchange(far_result, 2)
    back_cross = exchange(cross_result, 3)
    back_near = exchange(near_result, 1)
    shared_far, shared_near = after(shared_far, shared_near)
    relayed = exchange(shared_far, 1)
    shared_rows = call(shared_early_body, rows, pick, shared, shared_near, shared_far)
    steps = (0, 2, 3, 1)
    return call(
        functools.partial(last_body, steps),
        [whole] * 4,
        own_result,
        back_far,
        back_cross,
        relayed,
        back_near,
        last,
        turned_pick,
        shared_rows,
        out_specs=[in_hbm] * 4,
        scratch_shapes=[
            pltpu.VMEM(block.shape, BF16),
            pltpu.SemaphoreType.DMA((len(steps) + 1, 4)),
        ],
    )


def fold_blocks(step_fn, carried, arrays):
    count = arrays[0].shape[0]
    width = 512 if count % 512 == 0 else count
    blocks = tuple(
        (member.reshape((count // width, width) + member.shape[1:]) for member in arrays)
    )

    def inner_step(state, current):
        return (step_fn(state, current), None)

    result, unused = lax.scan(inner_step, carried, blocks)
    return result


def shards(queries, key_vectors, value_vectors, out_grad, keep_mask):
    win_count = lax.axis_size("win")
    win_index = lax.axis_index("win")
    tok_rows = queries.shape[1]
    feat_dev = queries.shape[2]
    head_count = feat_dev // HEAD_DIM
    slot_rows = tok_rows // win_count
    own_rows = tok_rows // 2
    inv_root = 1.0 / math.sqrt(HEAD_DIM)
    kept_flag = keep_mask[0]
    kept_here = jnp.sum(kept_flag)
    counts = lax.all_gather(kept_here.reshape(1), "win", axis=0, tiled=True)
    starts = jnp.cumsum(counts) - counts
    ends = starts + counts
    start_here = starts[win_index]
    kept_order = jnp.argsort(1 - kept_flag, stable=True)
    kept_rank = jnp.cumsum(kept_flag) - 1
    slot_index = jnp.arange(tok_rows, dtype=jnp.int32)
    target = slot_index // slot_rows
    within = slot_index % slot_rows
    leading = start_here + jnp.mod(target - start_here, win_count)
    global_pos = leading + within * win_count
    send_live = global_pos < start_here + kept_here
    send_rows = kept_order[jnp.clip(global_pos - start_here, 0, tok_rows - 1)]

    def pack(matrix):
        return jnp.where(send_live[:, None], matrix[0][send_rows], jnp.zeros((), matrix.dtype))

    own_index = jnp.arange(own_rows, dtype=jnp.int32)
    wanted = own_index * win_count + win_index
    source = jnp.sum((ends[None, :] <= wanted[:, None]).astype(jnp.int32), axis=1)
    source_start = starts[source]
    source_lead = source_start + jnp.mod(win_index - source_start, win_count)
    recv_rows = source * slot_rows + (wanted - source_lead) // win_count

    def unpack(matrix):
        return matrix[recv_rows]

    back_start = starts[target]
    back_lead = back_start + jnp.mod(win_index - back_start, win_count)
    back_global = back_lead + within * win_count
    back_live = back_global < ends[target]
    back_rows = jnp.clip(back_global // win_count, 0, own_rows - 1)

    def repack(matrix):
        return jnp.where(back_live[:, None], matrix[back_rows], jnp.zeros((), matrix.dtype))

    global_here = start_here + kept_rank
    owner = jnp.mod(global_here, win_count)
    owner_lead = start_here + jnp.mod(owner - start_here, win_count)
    land_rows = jnp.clip(
        owner * slot_rows + (global_here - owner_lead) // win_count, 0, tok_rows - 1
    )

    def place(matrix):
        return jnp.where(kept_flag[:, None] == 1, matrix[land_rows], jnp.zeros((), matrix.dtype))[
            None
        ]

    def heads_view(matrix):
        return matrix.reshape(matrix.shape[0], head_count, HEAD_DIM)

    got_query, got_key, got_value = (
        lax.all_to_all(pack(queries), "win", split_axis=0, concat_axis=0, tiled=True),
        lax.all_to_all(pack(key_vectors), "win", split_axis=0, concat_axis=0, tiled=True),
        lax.all_to_all(pack(value_vectors), "win", split_axis=0, concat_axis=0, tiled=True),
    )
    query_rows = unpack(got_query)
    key_rows = unpack(got_key)
    value_rows = unpack(got_value)
    query_heads = heads_view(query_rows)

    def soft_step(carried, current):
        highest, totals, summed = carried
        block_keys, block_values = current
        scores = (
            jnp.einsum(
                "qhe,khe->hqk",
                query_heads,
                heads_view(block_keys),
                preferred_element_type=jnp.float32,
            )
            * inv_root
        )
        peak_new = jnp.maximum(highest, jnp.max(scores, axis=-1))
        shrink = jnp.exp(highest - peak_new)
        raised = jnp.exp(scores - peak_new[..., None])
        totals = totals * shrink + jnp.sum(raised, axis=-1)
        summed = summed * shrink.T[..., None] + jnp.einsum(
            "hqk,khe->qhe",
            raised.astype(jnp.bfloat16),
            heads_view(block_values),
            preferred_element_type=jnp.float32,
        )
        return (peak_new, totals, summed)

    start_state = (
        jnp.full((head_count, own_rows), -jnp.inf, jnp.float32),
        jnp.zeros((head_count, own_rows), jnp.float32),
        jnp.zeros((own_rows, head_count, HEAD_DIM), jnp.float32),
    )
    highest, totals, summed = fold_blocks(
        soft_step,
        start_state,
        (
            lax.all_gather(key_rows, "win", axis=0, tiled=True),
            lax.all_gather(value_rows, "win", axis=0, tiled=True),
        ),
    )
    log_total = highest + jnp.log(totals)
    attended = (summed / totals.T[..., None]).astype(jnp.bfloat16)
    grad_rows = unpack(
        lax.all_to_all(pack(out_grad), "win", split_axis=0, concat_axis=0, tiled=True)
    )
    grad_heads = heads_view(grad_rows)
    inner = jnp.sum(grad_heads.astype(jnp.float32) * attended.astype(jnp.float32), axis=-1).T

    def query_step(carried, current):
        block_keys, block_values = current
        key_heads = heads_view(block_keys)
        scores = (
            jnp.einsum("qhe,khe->hqk", query_heads, key_heads, preferred_element_type=jnp.float32)
            * inv_root
        )
        weights = jnp.exp(scores - log_total[..., None]).astype(jnp.bfloat16)
        grad_scores = jnp.einsum(
            "qhe,khe->hqk", grad_heads, heads_view(block_values), preferred_element_type=jnp.float32
        )
        grad_logits = (
            weights.astype(jnp.float32) * (grad_scores - inner[..., None]) * inv_root
        ).astype(jnp.bfloat16)
        return carried + jnp.einsum(
            "hqk,khe->qhe", grad_logits, key_heads, preferred_element_type=jnp.float32
        )

    query_zero = jnp.zeros((own_rows, head_count, HEAD_DIM), jnp.float32)
    grad_query = fold_blocks(
        query_step,
        query_zero,
        (
            lax.all_gather(key_rows, "win", axis=0, tiled=True),
            lax.all_gather(value_rows, "win", axis=0, tiled=True),
        ),
    )
    all_log, all_inner = (
        lax.all_gather(log_total.T, "win", axis=0, tiled=True),
        lax.all_gather(inner.T, "win", axis=0, tiled=True),
    )
    own_key_heads = heads_view(key_rows)
    own_value_heads = heads_view(value_rows)

    def key_step(carried, current):
        key_total, value_total = carried
        block_queries, block_grads, block_log, block_inner = current
        query_block = heads_view(block_queries)
        grad_block = heads_view(block_grads)
        scores = (
            jnp.einsum(
                "khe,qhe->hkq", own_key_heads, query_block, preferred_element_type=jnp.float32
            )
            * inv_root
        )
        weights = jnp.exp(scores - block_log.T[:, None, :]).astype(jnp.bfloat16)
        value_total = value_total + jnp.einsum(
            "hkq,qhe->khe", weights, grad_block, preferred_element_type=jnp.float32
        )
        grad_scores = jnp.einsum(
            "khe,qhe->hkq", own_value_heads, grad_block, preferred_element_type=jnp.float32
        )
        grad_logits = (
            weights.astype(jnp.float32) * (grad_scores - block_inner.T[:, None, :]) * inv_root
        ).astype(jnp.bfloat16)
        key_total = key_total + jnp.einsum(
            "hkq,qhe->khe", grad_logits, query_block, preferred_element_type=jnp.float32
        )
        return (key_total, value_total)

    key_rows_count = key_rows.shape[0]
    empty_grads = jnp.zeros((key_rows_count, head_count, HEAD_DIM), jnp.float32)
    key_total, value_total = fold_blocks(
        key_step,
        (empty_grads, empty_grads),
        (
            lax.all_gather(query_rows, "win", axis=0, tiled=True),
            lax.all_gather(grad_rows, "win", axis=0, tiled=True),
            all_log,
            all_inner,
        ),
    )
    grad_key = key_total.reshape(key_rows_count, feat_dev).astype(jnp.bfloat16)
    grad_value = value_total.reshape(key_rows_count, feat_dev).astype(jnp.bfloat16)
    attended_flat = attended.reshape(own_rows, feat_dev)
    grad_query_flat = grad_query.reshape(own_rows, feat_dev).astype(jnp.bfloat16)
    back_attended, back_query, back_key, back_value = (
        lax.all_to_all(repack(attended_flat), "win", split_axis=0, concat_axis=0, tiled=True),
        lax.all_to_all(repack(grad_query_flat), "win", split_axis=0, concat_axis=0, tiled=True),
        lax.all_to_all(repack(grad_key), "win", split_axis=0, concat_axis=0, tiled=True),
        lax.all_to_all(repack(grad_value), "win", split_axis=0, concat_axis=0, tiled=True),
    )
    grad_key_out = place(back_key)
    grad_value_out = place(back_value)
    return (place(back_attended), place(back_query), grad_key_out, grad_value_out)


def by_plan(queries, key_vectors, value_vectors, out_grad, keep_mask):
    tokens, feat_dev = queries.shape[1:]
    dealt = lax.axis_size("win") == WINDOWS and feat_dev == (WINDOWS + 1) * HEAD_DIM
    run = shards_by_head if dealt and tokens == HEAD_DIM else shards
    return run(queries, key_vectors, value_vectors, out_grad, keep_mask)


def solution(mesh):
    placed = (
        P(("groups", "samp"), "win", "head"),
        P(("groups", "samp"), "win", "head"),
        P(("groups", "samp"), "win", "head"),
        P(("groups", "samp"), "win", "head"),
        P(("groups", "samp"), "win"),
    )
    return jax.shard_map(
        by_plan,
        mesh=mesh,
        in_specs=placed,
        out_specs=(
            P(("groups", "samp"), "win", "head"),
            P(("groups", "samp"), "win", "head"),
            P(("groups", "samp"), "win", "head"),
            P(("groups", "samp"), "win", "head"),
        ),
        check_vma=False,
    )
```

```python
import functools
import math

import jax
import jax.numpy as jnp
from jax import lax
from jax.experimental import pallas as pl
from jax.experimental.pallas import tpu as pltpu
from jax.sharding import PartitionSpec as P

HEAD_DIM = 128
TILE_ROWS = 16
WINDOWS = 4
DROPPED = 64.0
VMEM_BYTES = 16 << 20
BF16 = jnp.bfloat16
F32 = jnp.float32


def dot(left, right, left_dim=1, right_dim=0):
    return lax.dot_general(
        left, right, (((left_dim,), (right_dim,)), ((), ())), preferred_element_type=F32
    )


def attend_head(rows, needed=None):
    inv_root = 1.0 / math.sqrt(HEAD_DIM)
    needed = rows.shape[0] if needed is None else needed
    q, k, v, g = (rows[:, n * HEAD_DIM : (n + 1) * HEAD_DIM] for n in range(4))
    scores = dot(q, k, 1, 1) * inv_root
    grad_scores = dot(g, v, 1, 1)
    raised = jnp.exp(scores - jnp.max(scores, axis=1, keepdims=True))
    share = 1.0 / jnp.sum(raised, axis=1, keepdims=True)
    inner = jnp.sum(raised * grad_scores, axis=1, keepdims=True) * share
    weights = raised * share
    grad_logits = (weights * ((grad_scores - inner) * inv_root)).astype(BF16)
    weights = weights.astype(BF16)
    attended = (dot(raised[:needed].astype(BF16), v) * share[:needed]).astype(BF16)
    grad_q = dot(grad_logits[:needed], k).astype(BF16)
    grad_k = dot(grad_logits[:, :needed], q, 0, 0).astype(BF16)
    grad_v = dot(weights[:, :needed], g, 0, 0).astype(BF16)
    return jnp.concatenate([attended, grad_q, grad_k, grad_v], axis=1)


def side_by_side(ref):
    tokens = ref.shape[0] // 4
    return jnp.concatenate([ref[n * tokens : (n + 1) * tokens, :] for n in range(4)], axis=1)


def picks_of(blocks, kept, before):
    tokens = blocks[0].shape[0] // 4
    lead = (lax.broadcasted_iota(jnp.int32, (TILE_ROWS, HEAD_DIM), 1) == 0).astype(BF16)
    upto = (
        lax.broadcasted_iota(jnp.int32, (tokens, tokens), 0)
        <= lax.broadcasted_iota(jnp.int32, (tokens, tokens), 1)
    ).astype(BF16)
    slot = lax.broadcasted_iota(jnp.int32, (kept, tokens), 0).astype(F32)
    picks = []
    for block in blocks:
        live = dot(lead, block[0:tokens, :], 1, 1) < 0.5 * DROPPED
        rank = dot(live.astype(F32).astype(BF16), upto)[0:1]
        place = jnp.where(live[0:1], rank + (before - 1.0), -1.0)
        picks.append((slot == place).astype(F32).astype(BF16))
        before = before + rank[:, tokens - 1 : tokens]
    return jnp.concatenate(picks, axis=1), before


def put_back(out, picked, result):
    tokens = picked.shape[0]
    rows = dot(picked, result).astype(BF16)
    for n in range(4):
        out[n * tokens : (n + 1) * tokens, :] = rows[:, n * HEAD_DIM : (n + 1) * HEAD_DIM]


def head_lanes(head):
    if isinstance(head, int):
        return pl.ds(head * HEAD_DIM, HEAD_DIM)
    return pl.ds(pl.multiple_of(head * HEAD_DIM, HEAD_DIM), HEAD_DIM)


def pack_body(steps, q_ref, k_ref, v_ref, g_ref, mask_ref, *refs):
    outs, (mask_here, sems) = refs[:-2], refs[-2:]
    tokens = mask_ref.shape[1]
    me = lax.axis_index("win")
    copies = [pltpu.make_async_copy(mask_ref, mask_here, sems.at[0])]
    for out, step in zip(outs, steps):
        lanes = head_lanes(WINDOWS if step is None else me ^ step)
        for n, ref in enumerate((q_ref, k_ref, v_ref, g_ref)):
            copies.append(
                pltpu.make_async_copy(
                    ref.at[0, :, lanes],
                    out.at[n * tokens : (n + 1) * tokens, :],
                    sems.at[len(copies)],
                )
            )
    for copy in copies:
        copy.start()
    copies[0].wait()
    live = jnp.broadcast_to(mask_here[...].astype(F32), (TILE_ROWS, tokens)).astype(BF16)
    share = jnp.full((TILE_ROWS, HEAD_DIM), 1.0 / TILE_ROWS, BF16)
    keep = dot(live, share, 0, 0)
    mark = (1.0 - keep) * DROPPED
    for copy in copies[1:]:
        copy.wait()
    for out, step in zip(outs, steps):
        if step is not None:
            out[0:tokens, :] = (out[0:tokens, :].astype(F32) * keep + mark).astype(BF16)


def turned(pick):
    kept = pick.shape[0]
    unit = (
        lax.broadcasted_iota(jnp.int32, (kept, kept), 0)
        == lax.broadcasted_iota(jnp.int32, (kept, kept), 1)
    ).astype(F32).astype(BF16)
    return dot(pick, unit, 0, 0).astype(BF16)


def early_body(own, near, cross, pick_out, turned_out, rows_out, used_out):
    kept = pick_out.shape[0]
    blocks = (own, near, cross)
    pick, used = picks_of(blocks, kept, jnp.zeros((1, 1), F32))
    pick_out[...] = pick
    used_out[...] = jnp.broadcast_to(used, used_out.shape)
    rows_out[...] = dot(pick, jnp.concatenate([side_by_side(ref) for ref in blocks], axis=0)).astype(
        BF16
    )
    turned_out[...] = turned(pick)


def main_body(far, turned_ref, rows_ref, used_ref, own_out, near_out, far_out, cross_out, last_out):
    kept = rows_ref.shape[0]
    tokens = far.shape[0] // 4
    last, _ = picks_of((far,), kept, used_ref[0:1, 0:1])
    last_out[...] = last
    rows = rows_ref[...] + dot(last, side_by_side(far)).astype(BF16)
    result = attend_head(rows)
    put_back(far_out, turned(last), result)
    for n, out in ((1, near_out), (2, cross_out), (0, own_out)):
        put_back(out, turned_ref[n * tokens : (n + 1) * tokens, :], result)


def shared_early_body(pick_ref, last_ref, own, near, far, rows_out):
    tokens = last_ref.shape[1]
    pick = jnp.concatenate([pick_ref[:, 0 : 2 * tokens], last_ref[...]], axis=1)
    blocks = (own, near, far)
    rows_out[...] = dot(pick, jnp.concatenate([side_by_side(ref) for ref in blocks], axis=0)).astype(
        BF16
    )


def placed(back, tokens, lanes, outs, sems):
    return [
        pltpu.make_async_copy(
            back.at[n * tokens : (n + 1) * tokens, :], out.at[0, :, lanes], sems.at[n]
        )
        for n, out in enumerate(outs)
    ]


def last_body(steps, *refs):
    backs = list(refs[: len(steps) + 1])
    relayed = backs.pop(3)
    relpick_ref, turned_ref, rows_ref = refs[len(steps) + 1 : -6]
    outs, shared, sems = refs[-6:-2], refs[-2], refs[-1]
    tokens = outs[0].shape[1]
    me = lax.axis_index("win")
    copies = []
    for n, (back, step) in enumerate(zip(backs, steps)):
        copies += placed(back, tokens, head_lanes(me ^ step), outs, sems.at[n])
    for copy in copies:
        copy.start()
    rows = rows_ref[...] + dot(relpick_ref[:, 2 * tokens : 3 * tokens], side_by_side(relayed)).astype(BF16)
    put_back(shared, turned_ref[0:tokens, 0:tokens], attend_head(rows, tokens))
    more = placed(shared, tokens, head_lanes(WINDOWS), outs, sems.at[len(steps)])
    for copy in more:
        copy.start()
    for copy in copies + more:
        copy.wait()


def exchange(array, step):
    return lax.ppermute(array, "win", [(n, n ^ step) for n in range(WINDOWS)])


def after(array, other):
    return lax.optimization_barrier((array, other))


def shards_by_head(queries, key_vectors, value_vectors, out_grad, keep_mask):
    tokens = queries.shape[1]
    kept = WINDOWS * tokens // 2
    in_hbm = pl.BlockSpec(memory_space=pltpu.HBM)
    block = jax.ShapeDtypeStruct((4 * tokens, HEAD_DIM), BF16)
    rows = jax.ShapeDtypeStruct((kept, 4 * HEAD_DIM), BF16)
    turned_picks = jax.ShapeDtypeStruct((3 * tokens, kept), BF16)
    whole = jax.ShapeDtypeStruct(queries.shape, BF16)

    def picks(windows):
        return jax.ShapeDtypeStruct((kept, windows * tokens), BF16)

    def call(body, out_shape, *operands, flops=0, **specs):
        return pl.pallas_call(
            body,
            out_shape=out_shape,
            cost_estimate=pl.CostEstimate(flops=flops, bytes_accessed=0, transcendentals=0),
            compiler_params=pltpu.CompilerParams(vmem_limit_bytes=VMEM_BYTES),
            **specs,
        )(*operands)

    pinned = [
        pltpu.with_memory_space_constraint(one, pltpu.HBM)
        for one in (queries, key_vectors, value_vectors, out_grad, keep_mask)
    ]

    def pack(*steps):
        return call(
            functools.partial(pack_body, steps),
            [block] * len(steps),
            *pinned,
            in_specs=[in_hbm] * 5,
            scratch_shapes=[
                pltpu.VMEM(keep_mask.shape, keep_mask.dtype),
                pltpu.SemaphoreType.DMA((1 + 4 * len(steps),)),
            ],
        )

    (cross,) = pack(3)
    far, near, own, shared = pack(2, 1, 0, None)
    got_cross = exchange(cross, 3)
    got_far = exchange(far, 2)
    got_near = exchange(near, 1)
    late, got_cross = after(shared, got_cross)
    shared_far = exchange(late, 2)
    shared_near = exchange(late, 1)
    pick, turned_pick, some_rows, used = call(
        early_body,
        [picks(3), turned_picks, rows, jax.ShapeDtypeStruct((8, HEAD_DIM), F32)],
        own,
        got_near,
        got_cross,
        flops=1 << 28,
    )
    own_result, near_result, far_result, cross_result, last = call(
        main_body, [block] * 4 + [picks(1)], got_far, turned_pick, some_rows, used, flops=1 << 29
    )
    back_cross = exchange(cross_result, 3)
    back_far = exchange(far_result, 2)
    back_near = exchange(near_result, 1)
    shared_far, shared_near = after(shared_far, shared_near)
    relayed = exchange(shared_far, 1)
    shared_rows = call(shared_early_body, rows, pick, last, shared, shared_near, shared_far)
    steps = (0, 3, 2, 1)
    return call(
        functools.partial(last_body, steps),
        [whole] * 4,
        own_result,
        back_cross,
        back_far,
        relayed,
        back_near,
        pick,
        turned_pick,
        shared_rows,
        out_specs=[in_hbm] * 4,
        scratch_shapes=[
            pltpu.VMEM(block.shape, BF16),
            pltpu.SemaphoreType.DMA((len(steps) + 1, 4)),
        ],
    )


def fold_blocks(step_fn, carried, arrays):
    count = arrays[0].shape[0]
    width = 512 if count % 512 == 0 else count
    blocks = tuple(
        (member.reshape((count // width, width) + member.shape[1:]) for member in arrays)
    )

    def inner_step(state, current):
        return (step_fn(state, current), None)

    result, unused = lax.scan(inner_step, carried, blocks)
    return result


def shards(queries, key_vectors, value_vectors, out_grad, keep_mask):
    win_count = lax.axis_size("win")
    win_index = lax.axis_index("win")
    tok_rows = queries.shape[1]
    feat_dev = queries.shape[2]
    head_count = feat_dev // HEAD_DIM
    slot_rows = tok_rows // win_count
    own_rows = tok_rows // 2
    inv_root = 1.0 / math.sqrt(HEAD_DIM)
    kept_flag = keep_mask[0]
    kept_here = jnp.sum(kept_flag)
    counts = lax.all_gather(kept_here.reshape(1), "win", axis=0, tiled=True)
    starts = jnp.cumsum(counts) - counts
    ends = starts + counts
    start_here = starts[win_index]
    kept_order = jnp.argsort(1 - kept_flag, stable=True)
    kept_rank = jnp.cumsum(kept_flag) - 1
    slot_index = jnp.arange(tok_rows, dtype=jnp.int32)
    target = slot_index // slot_rows
    within = slot_index % slot_rows
    leading = start_here + jnp.mod(target - start_here, win_count)
    global_pos = leading + within * win_count
    send_live = global_pos < start_here + kept_here
    send_rows = kept_order[jnp.clip(global_pos - start_here, 0, tok_rows - 1)]

    def pack(matrix):
        return jnp.where(send_live[:, None], matrix[0][send_rows], jnp.zeros((), matrix.dtype))

    own_index = jnp.arange(own_rows, dtype=jnp.int32)
    wanted = own_index * win_count + win_index
    source = jnp.sum((ends[None, :] <= wanted[:, None]).astype(jnp.int32), axis=1)
    source_start = starts[source]
    source_lead = source_start + jnp.mod(win_index - source_start, win_count)
    recv_rows = source * slot_rows + (wanted - source_lead) // win_count

    def unpack(matrix):
        return matrix[recv_rows]

    back_start = starts[target]
    back_lead = back_start + jnp.mod(win_index - back_start, win_count)
    back_global = back_lead + within * win_count
    back_live = back_global < ends[target]
    back_rows = jnp.clip(back_global // win_count, 0, own_rows - 1)

    def repack(matrix):
        return jnp.where(back_live[:, None], matrix[back_rows], jnp.zeros((), matrix.dtype))

    global_here = start_here + kept_rank
    owner = jnp.mod(global_here, win_count)
    owner_lead = start_here + jnp.mod(owner - start_here, win_count)
    land_rows = jnp.clip(
        owner * slot_rows + (global_here - owner_lead) // win_count, 0, tok_rows - 1
    )

    def place(matrix):
        return jnp.where(kept_flag[:, None] == 1, matrix[land_rows], jnp.zeros((), matrix.dtype))[
            None
        ]

    def heads_view(matrix):
        return matrix.reshape(matrix.shape[0], head_count, HEAD_DIM)

    got_query, got_key, got_value = (
        lax.all_to_all(pack(queries), "win", split_axis=0, concat_axis=0, tiled=True),
        lax.all_to_all(pack(key_vectors), "win", split_axis=0, concat_axis=0, tiled=True),
        lax.all_to_all(pack(value_vectors), "win", split_axis=0, concat_axis=0, tiled=True),
    )
    query_rows = unpack(got_query)
    key_rows = unpack(got_key)
    value_rows = unpack(got_value)
    query_heads = heads_view(query_rows)

    def soft_step(carried, current):
        highest, totals, summed = carried
        block_keys, block_values = current
        scores = (
            jnp.einsum(
                "qhe,khe->hqk",
                query_heads,
                heads_view(block_keys),
                preferred_element_type=jnp.float32,
            )
            * inv_root
        )
        peak_new = jnp.maximum(highest, jnp.max(scores, axis=-1))
        shrink = jnp.exp(highest - peak_new)
        raised = jnp.exp(scores - peak_new[..., None])
        totals = totals * shrink + jnp.sum(raised, axis=-1)
        summed = summed * shrink.T[..., None] + jnp.einsum(
            "hqk,khe->qhe",
            raised.astype(jnp.bfloat16),
            heads_view(block_values),
            preferred_element_type=jnp.float32,
        )
        return (peak_new, totals, summed)

    start_state = (
        jnp.full((head_count, own_rows), -jnp.inf, jnp.float32),
        jnp.zeros((head_count, own_rows), jnp.float32),
        jnp.zeros((own_rows, head_count, HEAD_DIM), jnp.float32),
    )
    highest, totals, summed = fold_blocks(
        soft_step,
        start_state,
        (
            lax.all_gather(key_rows, "win", axis=0, tiled=True),
            lax.all_gather(value_rows, "win", axis=0, tiled=True),
        ),
    )
    log_total = highest + jnp.log(totals)
    attended = (summed / totals.T[..., None]).astype(jnp.bfloat16)
    grad_rows = unpack(
        lax.all_to_all(pack(out_grad), "win", split_axis=0, concat_axis=0, tiled=True)
    )
    grad_heads = heads_view(grad_rows)
    inner = jnp.sum(grad_heads.astype(jnp.float32) * attended.astype(jnp.float32), axis=-1).T

    def query_step(carried, current):
        block_keys, block_values = current
        key_heads = heads_view(block_keys)
        scores = (
            jnp.einsum("qhe,khe->hqk", query_heads, key_heads, preferred_element_type=jnp.float32)
            * inv_root
        )
        weights = jnp.exp(scores - log_total[..., None]).astype(jnp.bfloat16)
        grad_scores = jnp.einsum(
            "qhe,khe->hqk", grad_heads, heads_view(block_values), preferred_element_type=jnp.float32
        )
        grad_logits = (
            weights.astype(jnp.float32) * (grad_scores - inner[..., None]) * inv_root
        ).astype(jnp.bfloat16)
        return carried + jnp.einsum(
            "hqk,khe->qhe", grad_logits, key_heads, preferred_element_type=jnp.float32
        )

    query_zero = jnp.zeros((own_rows, head_count, HEAD_DIM), jnp.float32)
    grad_query = fold_blocks(
        query_step,
        query_zero,
        (
            lax.all_gather(key_rows, "win", axis=0, tiled=True),
            lax.all_gather(value_rows, "win", axis=0, tiled=True),
        ),
    )
    all_log, all_inner = (
        lax.all_gather(log_total.T, "win", axis=0, tiled=True),
        lax.all_gather(inner.T, "win", axis=0, tiled=True),
    )
    own_key_heads = heads_view(key_rows)
    own_value_heads = heads_view(value_rows)

    def key_step(carried, current):
        key_total, value_total = carried
        block_queries, block_grads, block_log, block_inner = current
        query_block = heads_view(block_queries)
        grad_block = heads_view(block_grads)
        scores = (
            jnp.einsum(
                "khe,qhe->hkq", own_key_heads, query_block, preferred_element_type=jnp.float32
            )
            * inv_root
        )
        weights = jnp.exp(scores - block_log.T[:, None, :]).astype(jnp.bfloat16)
        value_total = value_total + jnp.einsum(
            "hkq,qhe->khe", weights, grad_block, preferred_element_type=jnp.float32
        )
        grad_scores = jnp.einsum(
            "khe,qhe->hkq", own_value_heads, grad_block, preferred_element_type=jnp.float32
        )
        grad_logits = (
            weights.astype(jnp.float32) * (grad_scores - block_inner.T[:, None, :]) * inv_root
        ).astype(jnp.bfloat16)
        key_total = key_total + jnp.einsum(
            "hkq,qhe->khe", grad_logits, query_block, preferred_element_type=jnp.float32
        )
        return (key_total, value_total)

    key_rows_count = key_rows.shape[0]
    empty_grads = jnp.zeros((key_rows_count, head_count, HEAD_DIM), jnp.float32)
    key_total, value_total = fold_blocks(
        key_step,
        (empty_grads, empty_grads),
        (
            lax.all_gather(query_rows, "win", axis=0, tiled=True),
            lax.all_gather(grad_rows, "win", axis=0, tiled=True),
            all_log,
            all_inner,
        ),
    )
    grad_key = key_total.reshape(key_rows_count, feat_dev).astype(jnp.bfloat16)
    grad_value = value_total.reshape(key_rows_count, feat_dev).astype(jnp.bfloat16)
    attended_flat = attended.reshape(own_rows, feat_dev)
    grad_query_flat = grad_query.reshape(own_rows, feat_dev).astype(jnp.bfloat16)
    back_attended, back_query, back_key, back_value = (
        lax.all_to_all(repack(attended_flat), "win", split_axis=0, concat_axis=0, tiled=True),
        lax.all_to_all(repack(grad_query_flat), "win", split_axis=0, concat_axis=0, tiled=True),
        lax.all_to_all(repack(grad_key), "win", split_axis=0, concat_axis=0, tiled=True),
        lax.all_to_all(repack(grad_value), "win", split_axis=0, concat_axis=0, tiled=True),
    )
    grad_key_out = place(back_key)
    grad_value_out = place(back_value)
    return (place(back_attended), place(back_query), grad_key_out, grad_value_out)


def by_plan(queries, key_vectors, value_vectors, out_grad, keep_mask):
    tokens, feat_dev = queries.shape[1:]
    dealt = lax.axis_size("win") == WINDOWS and feat_dev == (WINDOWS + 1) * HEAD_DIM
    run = shards_by_head if dealt and tokens == HEAD_DIM else shards
    return run(queries, key_vectors, value_vectors, out_grad, keep_mask)


def solution(mesh):
    placed = (
        P(("groups", "samp"), "win", "head"),
        P(("groups", "samp"), "win", "head"),
        P(("groups", "samp"), "win", "head"),
        P(("groups", "samp"), "win", "head"),
        P(("groups", "samp"), "win"),
    )
    return jax.shard_map(
        by_plan,
        mesh=mesh,
        in_specs=placed,
        out_specs=(
            P(("groups", "samp"), "win", "head"),
            P(("groups", "samp"), "win", "head"),
            P(("groups", "samp"), "win", "head"),
            P(("groups", "samp"), "win", "head"),
        ),
        check_vma=False,
    )
```

```python
import functools
import math

import jax
import jax.numpy as jnp
from jax import lax
from jax.experimental import pallas as pl
from jax.experimental.pallas import tpu as pltpu
from jax.sharding import PartitionSpec as P

HEAD_DIM = 128
TILE_ROWS = 16
WINDOWS = 4
DROPPED = 64.0
VMEM_BYTES = 16 << 20
BF16 = jnp.bfloat16
F32 = jnp.float32


def dot(left, right, left_dim=1, right_dim=0):
    return lax.dot_general(
        left, right, (((left_dim,), (right_dim,)), ((), ())), preferred_element_type=F32
    )


def attend_head(rows, needed=None):
    inv_root = 1.0 / math.sqrt(HEAD_DIM)
    needed = rows.shape[0] if needed is None else needed
    q, k, v, g = (rows[:, n * HEAD_DIM : (n + 1) * HEAD_DIM] for n in range(4))
    scores = dot(q, k, 1, 1) * inv_root
    grad_scores = dot(g, v, 1, 1)
    raised = jnp.exp(scores - jnp.max(scores, axis=1, keepdims=True))
    share = 1.0 / jnp.sum(raised, axis=1, keepdims=True)
    inner = jnp.sum(raised * grad_scores, axis=1, keepdims=True) * share
    weights = raised * share
    grad_logits = (weights * ((grad_scores - inner) * inv_root)).astype(BF16)
    weights = weights.astype(BF16)
    attended = (dot(raised[:needed].astype(BF16), v) * share[:needed]).astype(BF16)
    grad_q = dot(grad_logits[:needed], k).astype(BF16)
    grad_k = dot(grad_logits[:, :needed], q, 0, 0).astype(BF16)
    grad_v = dot(weights[:, :needed], g, 0, 0).astype(BF16)
    return jnp.concatenate([attended, grad_q, grad_k, grad_v], axis=1)


def side_by_side(ref):
    tokens = ref.shape[0] // 4
    return jnp.concatenate([ref[n * tokens : (n + 1) * tokens, :] for n in range(4)], axis=1)


def picks_of(blocks, kept, before):
    tokens = blocks[0].shape[0] // 4
    lead = (lax.broadcasted_iota(jnp.int32, (TILE_ROWS, HEAD_DIM), 1) == 0).astype(BF16)
    upto = (
        lax.broadcasted_iota(jnp.int32, (tokens, tokens), 0)
        <= lax.broadcasted_iota(jnp.int32, (tokens, tokens), 1)
    ).astype(BF16)
    slot = lax.broadcasted_iota(jnp.int32, (kept, tokens), 0).astype(F32)
    picks = []
    for block in blocks:
        live = dot(lead, block[0:tokens, :], 1, 1) < 0.5 * DROPPED
        rank = dot(live.astype(F32).astype(BF16), upto)[0:1]
        place = jnp.where(live[0:1], rank + (before - 1.0), -1.0)
        picks.append((slot == place).astype(F32).astype(BF16))
        before = before + rank[:, tokens - 1 : tokens]
    return jnp.concatenate(picks, axis=1), before


def put_back(out, picked, result):
    tokens = picked.shape[0]
    rows = dot(picked, result).astype(BF16)
    for n in range(4):
        out[n * tokens : (n + 1) * tokens, :] = rows[:, n * HEAD_DIM : (n + 1) * HEAD_DIM]


def head_lanes(head):
    if isinstance(head, int):
        return pl.ds(head * HEAD_DIM, HEAD_DIM)
    return pl.ds(pl.multiple_of(head * HEAD_DIM, HEAD_DIM), HEAD_DIM)


def pack_body(steps, q_ref, k_ref, v_ref, g_ref, mask_ref, *refs):
    outs, (mask_here, sems) = refs[:-2], refs[-2:]
    tokens = mask_ref.shape[1]
    me = lax.axis_index("win")
    copies = [pltpu.make_async_copy(mask_ref, mask_here, sems.at[0])]
    for out, step in zip(outs, steps):
        lanes = head_lanes(WINDOWS if step is None else me ^ step)
        for n, ref in enumerate((q_ref, k_ref, v_ref, g_ref)):
            copies.append(
                pltpu.make_async_copy(
                    ref.at[0, :, lanes],
                    out.at[n * tokens : (n + 1) * tokens, :],
                    sems.at[len(copies)],
                )
            )
    for copy in copies:
        copy.start()
    copies[0].wait()
    live = jnp.broadcast_to(mask_here[...].astype(F32), (TILE_ROWS, tokens)).astype(BF16)
    share = jnp.full((TILE_ROWS, HEAD_DIM), 1.0 / TILE_ROWS, BF16)
    keep = dot(live, share, 0, 0)
    mark = (1.0 - keep) * DROPPED
    for copy in copies[1:]:
        copy.wait()
    for out, step in zip(outs, steps):
        if step is not None:
            out[0:tokens, :] = (out[0:tokens, :].astype(F32) * keep + mark).astype(BF16)


def turned(pick):
    kept = pick.shape[0]
    unit = (
        lax.broadcasted_iota(jnp.int32, (kept, kept), 0)
        == lax.broadcasted_iota(jnp.int32, (kept, kept), 1)
    ).astype(F32).astype(BF16)
    return dot(pick, unit, 0, 0).astype(BF16)


def early_body(own, near, cross, pick_out, turned_out, rows_out, used_out):
    kept = pick_out.shape[0]
    blocks = (own, near, cross)
    pick, used = picks_of(blocks, kept, jnp.zeros((1, 1), F32))
    pick_out[...] = pick
    used_out[...] = jnp.broadcast_to(used, used_out.shape)
    rows_out[...] = dot(pick, jnp.concatenate([side_by_side(ref) for ref in blocks], axis=0)).astype(
        BF16
    )
    turned_out[...] = turned(pick)


def main_body(far, turned_ref, rows_ref, used_ref, own_out, near_out, far_out, cross_out, last_out):
    kept = rows_ref.shape[0]
    tokens = far.shape[0] // 4
    last, _ = picks_of((far,), kept, used_ref[0:1, 0:1])
    last_out[...] = last
    rows = rows_ref[...] + dot(last, side_by_side(far)).astype(BF16)
    result = attend_head(rows)
    put_back(far_out, turned(last), result)
    for n, out in ((1, near_out), (2, cross_out), (0, own_out)):
        put_back(out, turned_ref[n * tokens : (n + 1) * tokens, :], result)


def shared_body(pick_ref, last_ref, turned_ref, own, near, cross, far, own_out, near_out):
    tokens = last_ref.shape[1]
    pick = jnp.concatenate([pick_ref[...], last_ref[...]], axis=1)
    blocks = (own, near, cross, far)
    rows = dot(pick, jnp.concatenate([side_by_side(ref) for ref in blocks], axis=0)).astype(BF16)
    result = attend_head(rows)
    put_back(own_out, turned_ref[0:tokens, :], result)
    put_back(near_out, turned_ref[tokens : 2 * tokens, :], result)


def placed(back, tokens, lanes, outs, sems):
    return [
        pltpu.make_async_copy(
            back.at[n * tokens : (n + 1) * tokens, :], out.at[0, :, lanes], sems.at[n]
        )
        for n, out in enumerate(outs)
    ]


def last_body(steps, *refs):
    backs, (shared_here, shared_there) = refs[: len(steps)], refs[len(steps) : -6]
    outs, shared, sems = refs[-6:-2], refs[-2], refs[-1]
    tokens = outs[0].shape[1]
    me = lax.axis_index("win")
    copies = []
    for n, (back, step) in enumerate(zip(backs, steps)):
        copies += placed(back, tokens, head_lanes(me ^ step), outs, sems.at[n])
    for copy in copies:
        copy.start()
    at_end = jnp.logical_or(me == 0, me == WINDOWS - 1)

    @pl.when(at_end)
    def _():
        shared[...] = shared_there[...]

    @pl.when(jnp.logical_not(at_end))
    def _():
        shared[...] = shared_here[...]

    more = placed(shared, tokens, head_lanes(WINDOWS), outs, sems.at[len(steps)])
    for copy in more:
        copy.start()
    for copy in copies + more:
        copy.wait()


def exchange(array, step):
    return lax.ppermute(array, "win", [(n, n ^ step) for n in range(WINDOWS)])


def along(array, *pairs):
    return lax.ppermute(array, "win", pairs)


def after(array, other):
    return lax.optimization_barrier((array, other))


def shards_by_head(queries, key_vectors, value_vectors, out_grad, keep_mask):
    tokens = queries.shape[1]
    kept = WINDOWS * tokens // 2
    in_hbm = pl.BlockSpec(memory_space=pltpu.HBM)
    block = jax.ShapeDtypeStruct((4 * tokens, HEAD_DIM), BF16)
    rows = jax.ShapeDtypeStruct((kept, 4 * HEAD_DIM), BF16)
    turned_picks = jax.ShapeDtypeStruct((3 * tokens, kept), BF16)
    whole = jax.ShapeDtypeStruct(queries.shape, BF16)

    def picks(windows):
        return jax.ShapeDtypeStruct((kept, windows * tokens), BF16)

    def call(body, out_shape, *operands, flops=0, **specs):
        return pl.pallas_call(
            body,
            out_shape=out_shape,
            cost_estimate=pl.CostEstimate(flops=flops, bytes_accessed=0, transcendentals=0),
            compiler_params=pltpu.CompilerParams(vmem_limit_bytes=VMEM_BYTES),
            **specs,
        )(*operands)

    pinned = [
        pltpu.with_memory_space_constraint(one, pltpu.HBM)
        for one in (queries, key_vectors, value_vectors, out_grad, keep_mask)
    ]

    def pack(*steps):
        return call(
            functools.partial(pack_body, steps),
            [block] * len(steps),
            *pinned,
            in_specs=[in_hbm] * 5,
            scratch_shapes=[
                pltpu.VMEM(keep_mask.shape, keep_mask.dtype),
                pltpu.SemaphoreType.DMA((1 + 4 * len(steps),)),
            ],
        )

    (cross,) = pack(3)
    far, near, own, shared = pack(2, 1, 0, None)
    got_cross = exchange(cross, 3)
    got_far = exchange(far, 2)
    got_near = exchange(near, 1)
    late, got_cross = after(shared, got_cross)
    shared_near = along(shared, (0, 1), (3, 2))
    shared_cross = along(late, (1, 2), (2, 1))
    shared_far = along(shared_near, (1, 2), (2, 1))
    pick, turned_pick, some_rows, used = call(
        early_body,
        [picks(3), turned_picks, rows, jax.ShapeDtypeStruct((8, HEAD_DIM), F32)],
        own,
        got_near,
        got_cross,
        flops=1 << 28,
    )
    own_result, near_result, far_result, cross_result, last = call(
        main_body, [block] * 4 + [picks(1)], got_far, turned_pick, some_rows, used, flops=1 << 29
    )
    back_near = exchange(near_result, 1)
    back_cross = exchange(cross_result, 3)
    back_far = exchange(far_result, 2)
    shared_here, for_near = call(
        shared_body,
        [block] * 2,
        pick,
        last,
        turned_pick,
        shared,
        shared_near,
        shared_cross,
        shared_far,
    )
    shared_there = along(for_near, (1, 0), (2, 3))
    steps = (0, 1, 3, 2)
    return call(
        functools.partial(last_body, steps),
        [whole] * 4,
        own_result,
        back_near,
        back_cross,
        back_far,
        shared_here,
        shared_there,
        out_specs=[in_hbm] * 4,
        scratch_shapes=[
            pltpu.VMEM(block.shape, BF16),
            pltpu.SemaphoreType.DMA((len(steps) + 1, 4)),
        ],
    )


def fold_blocks(step_fn, carried, arrays):
    count = arrays[0].shape[0]
    width = 512 if count % 512 == 0 else count
    blocks = tuple(
        (member.reshape((count // width, width) + member.shape[1:]) for member in arrays)
    )

    def inner_step(state, current):
        return (step_fn(state, current), None)

    result, unused = lax.scan(inner_step, carried, blocks)
    return result


def shards(queries, key_vectors, value_vectors, out_grad, keep_mask):
    win_count = lax.axis_size("win")
    win_index = lax.axis_index("win")
    tok_rows = queries.shape[1]
    feat_dev = queries.shape[2]
    head_count = feat_dev // HEAD_DIM
    slot_rows = tok_rows // win_count
    own_rows = tok_rows // 2
    inv_root = 1.0 / math.sqrt(HEAD_DIM)
    kept_flag = keep_mask[0]
    kept_here = jnp.sum(kept_flag)
    counts = lax.all_gather(kept_here.reshape(1), "win", axis=0, tiled=True)
    starts = jnp.cumsum(counts) - counts
    ends = starts + counts
    start_here = starts[win_index]
    kept_order = jnp.argsort(1 - kept_flag, stable=True)
    kept_rank = jnp.cumsum(kept_flag) - 1
    slot_index = jnp.arange(tok_rows, dtype=jnp.int32)
    target = slot_index // slot_rows
    within = slot_index % slot_rows
    leading = start_here + jnp.mod(target - start_here, win_count)
    global_pos = leading + within * win_count
    send_live = global_pos < start_here + kept_here
    send_rows = kept_order[jnp.clip(global_pos - start_here, 0, tok_rows - 1)]

    def pack(matrix):
        return jnp.where(send_live[:, None], matrix[0][send_rows], jnp.zeros((), matrix.dtype))

    own_index = jnp.arange(own_rows, dtype=jnp.int32)
    wanted = own_index * win_count + win_index
    source = jnp.sum((ends[None, :] <= wanted[:, None]).astype(jnp.int32), axis=1)
    source_start = starts[source]
    source_lead = source_start + jnp.mod(win_index - source_start, win_count)
    recv_rows = source * slot_rows + (wanted - source_lead) // win_count

    def unpack(matrix):
        return matrix[recv_rows]

    back_start = starts[target]
    back_lead = back_start + jnp.mod(win_index - back_start, win_count)
    back_global = back_lead + within * win_count
    back_live = back_global < ends[target]
    back_rows = jnp.clip(back_global // win_count, 0, own_rows - 1)

    def repack(matrix):
        return jnp.where(back_live[:, None], matrix[back_rows], jnp.zeros((), matrix.dtype))

    global_here = start_here + kept_rank
    owner = jnp.mod(global_here, win_count)
    owner_lead = start_here + jnp.mod(owner - start_here, win_count)
    land_rows = jnp.clip(
        owner * slot_rows + (global_here - owner_lead) // win_count, 0, tok_rows - 1
    )

    def place(matrix):
        return jnp.where(kept_flag[:, None] == 1, matrix[land_rows], jnp.zeros((), matrix.dtype))[
            None
        ]

    def heads_view(matrix):
        return matrix.reshape(matrix.shape[0], head_count, HEAD_DIM)

    got_query, got_key, got_value = (
        lax.all_to_all(pack(queries), "win", split_axis=0, concat_axis=0, tiled=True),
        lax.all_to_all(pack(key_vectors), "win", split_axis=0, concat_axis=0, tiled=True),
        lax.all_to_all(pack(value_vectors), "win", split_axis=0, concat_axis=0, tiled=True),
    )
    query_rows = unpack(got_query)
    key_rows = unpack(got_key)
    value_rows = unpack(got_value)
    query_heads = heads_view(query_rows)

    def soft_step(carried, current):
        highest, totals, summed = carried
        block_keys, block_values = current
        scores = (
            jnp.einsum(
                "qhe,khe->hqk",
                query_heads,
                heads_view(block_keys),
                preferred_element_type=jnp.float32,
            )
            * inv_root
        )
        peak_new = jnp.maximum(highest, jnp.max(scores, axis=-1))
        shrink = jnp.exp(highest - peak_new)
        raised = jnp.exp(scores - peak_new[..., None])
        totals = totals * shrink + jnp.sum(raised, axis=-1)
        summed = summed * shrink.T[..., None] + jnp.einsum(
            "hqk,khe->qhe",
            raised.astype(jnp.bfloat16),
            heads_view(block_values),
            preferred_element_type=jnp.float32,
        )
        return (peak_new, totals, summed)

    start_state = (
        jnp.full((head_count, own_rows), -jnp.inf, jnp.float32),
        jnp.zeros((head_count, own_rows), jnp.float32),
        jnp.zeros((own_rows, head_count, HEAD_DIM), jnp.float32),
    )
    highest, totals, summed = fold_blocks(
        soft_step,
        start_state,
        (
            lax.all_gather(key_rows, "win", axis=0, tiled=True),
            lax.all_gather(value_rows, "win", axis=0, tiled=True),
        ),
    )
    log_total = highest + jnp.log(totals)
    attended = (summed / totals.T[..., None]).astype(jnp.bfloat16)
    grad_rows = unpack(
        lax.all_to_all(pack(out_grad), "win", split_axis=0, concat_axis=0, tiled=True)
    )
    grad_heads = heads_view(grad_rows)
    inner = jnp.sum(grad_heads.astype(jnp.float32) * attended.astype(jnp.float32), axis=-1).T

    def query_step(carried, current):
        block_keys, block_values = current
        key_heads = heads_view(block_keys)
        scores = (
            jnp.einsum("qhe,khe->hqk", query_heads, key_heads, preferred_element_type=jnp.float32)
            * inv_root
        )
        weights = jnp.exp(scores - log_total[..., None]).astype(jnp.bfloat16)
        grad_scores = jnp.einsum(
            "qhe,khe->hqk", grad_heads, heads_view(block_values), preferred_element_type=jnp.float32
        )
        grad_logits = (
            weights.astype(jnp.float32) * (grad_scores - inner[..., None]) * inv_root
        ).astype(jnp.bfloat16)
        return carried + jnp.einsum(
            "hqk,khe->qhe", grad_logits, key_heads, preferred_element_type=jnp.float32
        )

    query_zero = jnp.zeros((own_rows, head_count, HEAD_DIM), jnp.float32)
    grad_query = fold_blocks(
        query_step,
        query_zero,
        (
            lax.all_gather(key_rows, "win", axis=0, tiled=True),
            lax.all_gather(value_rows, "win", axis=0, tiled=True),
        ),
    )
    all_log, all_inner = (
        lax.all_gather(log_total.T, "win", axis=0, tiled=True),
        lax.all_gather(inner.T, "win", axis=0, tiled=True),
    )
    own_key_heads = heads_view(key_rows)
    own_value_heads = heads_view(value_rows)

    def key_step(carried, current):
        key_total, value_total = carried
        block_queries, block_grads, block_log, block_inner = current
        query_block = heads_view(block_queries)
        grad_block = heads_view(block_grads)
        scores = (
            jnp.einsum(
                "khe,qhe->hkq", own_key_heads, query_block, preferred_element_type=jnp.float32
            )
            * inv_root
        )
        weights = jnp.exp(scores - block_log.T[:, None, :]).astype(jnp.bfloat16)
        value_total = value_total + jnp.einsum(
            "hkq,qhe->khe", weights, grad_block, preferred_element_type=jnp.float32
        )
        grad_scores = jnp.einsum(
            "khe,qhe->hkq", own_value_heads, grad_block, preferred_element_type=jnp.float32
        )
        grad_logits = (
            weights.astype(jnp.float32) * (grad_scores - block_inner.T[:, None, :]) * inv_root
        ).astype(jnp.bfloat16)
        key_total = key_total + jnp.einsum(
            "hkq,qhe->khe", grad_logits, query_block, preferred_element_type=jnp.float32
        )
        return (key_total, value_total)

    key_rows_count = key_rows.shape[0]
    empty_grads = jnp.zeros((key_rows_count, head_count, HEAD_DIM), jnp.float32)
    key_total, value_total = fold_blocks(
        key_step,
        (empty_grads, empty_grads),
        (
            lax.all_gather(query_rows, "win", axis=0, tiled=True),
            lax.all_gather(grad_rows, "win", axis=0, tiled=True),
            all_log,
            all_inner,
        ),
    )
    grad_key = key_total.reshape(key_rows_count, feat_dev).astype(jnp.bfloat16)
    grad_value = value_total.reshape(key_rows_count, feat_dev).astype(jnp.bfloat16)
    attended_flat = attended.reshape(own_rows, feat_dev)
    grad_query_flat = grad_query.reshape(own_rows, feat_dev).astype(jnp.bfloat16)
    back_attended, back_query, back_key, back_value = (
        lax.all_to_all(repack(attended_flat), "win", split_axis=0, concat_axis=0, tiled=True),
        lax.all_to_all(repack(grad_query_flat), "win", split_axis=0, concat_axis=0, tiled=True),
        lax.all_to_all(repack(grad_key), "win", split_axis=0, concat_axis=0, tiled=True),
        lax.all_to_all(repack(grad_value), "win", split_axis=0, concat_axis=0, tiled=True),
    )
    grad_key_out = place(back_key)
    grad_value_out = place(back_value)
    return (place(back_attended), place(back_query), grad_key_out, grad_value_out)


def by_plan(queries, key_vectors, value_vectors, out_grad, keep_mask):
    tokens, feat_dev = queries.shape[1:]
    dealt = lax.axis_size("win") == WINDOWS and feat_dev == (WINDOWS + 1) * HEAD_DIM
    run = shards_by_head if dealt and tokens == HEAD_DIM else shards
    return run(queries, key_vectors, value_vectors, out_grad, keep_mask)


def solution(mesh):
    placed = (
        P(("groups", "samp"), "win", "head"),
        P(("groups", "samp"), "win", "head"),
        P(("groups", "samp"), "win", "head"),
        P(("groups", "samp"), "win", "head"),
        P(("groups", "samp"), "win"),
    )
    return jax.shard_map(
        by_plan,
        mesh=mesh,
        in_specs=placed,
        out_specs=(
            P(("groups", "samp"), "win", "head"),
            P(("groups", "samp"), "win", "head"),
            P(("groups", "samp"), "win", "head"),
            P(("groups", "samp"), "win", "head"),
        ),
        check_vma=False,
    )
```

```python
import functools
import math

import jax
import jax.numpy as jnp
from jax import lax
from jax.experimental import pallas as pl
from jax.experimental.pallas import tpu as pltpu
from jax.sharding import PartitionSpec as P

HEAD_DIM = 128
TILE_ROWS = 16
WINDOWS = 4
DROPPED = 64.0
VMEM_BYTES = 16 << 20
BF16 = jnp.bfloat16
F32 = jnp.float32


def dot(left, right, left_dim=1, right_dim=0):
    return lax.dot_general(
        left, right, (((left_dim,), (right_dim,)), ((), ())), preferred_element_type=F32
    )


def attend_head(rows, needed=None):
    inv_root = 1.0 / math.sqrt(HEAD_DIM)
    needed = rows.shape[0] if needed is None else needed
    q, k, v, g = (rows[:, n * HEAD_DIM : (n + 1) * HEAD_DIM] for n in range(4))
    scores = dot(q, k, 1, 1) * inv_root
    grad_scores = dot(g, v, 1, 1)
    raised = jnp.exp(scores - jnp.max(scores, axis=1, keepdims=True))
    share = 1.0 / jnp.sum(raised, axis=1, keepdims=True)
    inner = jnp.sum(raised * grad_scores, axis=1, keepdims=True) * share
    weights = raised * share
    grad_logits = (weights * ((grad_scores - inner) * inv_root)).astype(BF16)
    weights = weights.astype(BF16)
    attended = (dot(raised[:needed].astype(BF16), v) * share[:needed]).astype(BF16)
    grad_q = dot(grad_logits[:needed], k).astype(BF16)
    grad_k = dot(grad_logits[:, :needed], q, 0, 0).astype(BF16)
    grad_v = dot(weights[:, :needed], g, 0, 0).astype(BF16)
    return jnp.concatenate([attended, grad_q, grad_k, grad_v], axis=1)


def side_by_side(ref):
    tokens = ref.shape[0] // 4
    return jnp.concatenate([ref[n * tokens : (n + 1) * tokens, :] for n in range(4)], axis=1)


def picks_of(blocks, kept, before):
    tokens = blocks[0].shape[0] // 4
    lead = (lax.broadcasted_iota(jnp.int32, (TILE_ROWS, HEAD_DIM), 1) == 0).astype(BF16)
    upto = (
        lax.broadcasted_iota(jnp.int32, (tokens, tokens), 0)
        <= lax.broadcasted_iota(jnp.int32, (tokens, tokens), 1)
    ).astype(BF16)
    slot = lax.broadcasted_iota(jnp.int32, (kept, tokens), 0).astype(F32)
    picks = []
    for block in blocks:
        live = dot(lead, block[0:tokens, :], 1, 1) < 0.5 * DROPPED
        rank = dot(live.astype(F32).astype(BF16), upto)[0:1]
        place = jnp.where(live[0:1], rank + (before - 1.0), -1.0)
        picks.append((slot == place).astype(F32).astype(BF16))
        before = before + rank[:, tokens - 1 : tokens]
    return jnp.concatenate(picks, axis=1), before


def put_back(out, picked, result):
    tokens = picked.shape[0]
    rows = dot(picked, result).astype(BF16)
    for n in range(4):
        out[n * tokens : (n + 1) * tokens, :] = rows[:, n * HEAD_DIM : (n + 1) * HEAD_DIM]


def head_lanes(head):
    if isinstance(head, int):
        return pl.ds(head * HEAD_DIM, HEAD_DIM)
    return pl.ds(pl.multiple_of(head * HEAD_DIM, HEAD_DIM), HEAD_DIM)


def pack_body(steps, q_ref, k_ref, v_ref, g_ref, mask_ref, *refs):
    outs, (mask_here, sems) = refs[:-2], refs[-2:]
    tokens = mask_ref.shape[1]
    me = lax.axis_index("win")
    copies = [pltpu.make_async_copy(mask_ref, mask_here, sems.at[0])]
    for out, step in zip(outs, steps):
        lanes = head_lanes(WINDOWS if step is None else me ^ step)
        for n, ref in enumerate((q_ref, k_ref, v_ref, g_ref)):
            copies.append(
                pltpu.make_async_copy(
                    ref.at[0, :, lanes],
                    out.at[n * tokens : (n + 1) * tokens, :],
                    sems.at[len(copies)],
                )
            )
    for copy in copies:
        copy.start()
    copies[0].wait()
    live = jnp.broadcast_to(mask_here[...].astype(F32), (TILE_ROWS, tokens)).astype(BF16)
    share = jnp.full((TILE_ROWS, HEAD_DIM), 1.0 / TILE_ROWS, BF16)
    keep = dot(live, share, 0, 0)
    mark = (1.0 - keep) * DROPPED
    for copy in copies[1:]:
        copy.wait()
    for out, step in zip(outs, steps):
        if step is not None:
            out[0:tokens, :] = (out[0:tokens, :].astype(F32) * keep + mark).astype(BF16)


def turned(pick):
    kept = pick.shape[0]
    unit = (
        lax.broadcasted_iota(jnp.int32, (kept, kept), 0)
        == lax.broadcasted_iota(jnp.int32, (kept, kept), 1)
    ).astype(F32).astype(BF16)
    return dot(pick, unit, 0, 0).astype(BF16)


def early_body(own, near, cross, pick_out, turned_out, rows_out, used_out):
    kept = pick_out.shape[0]
    blocks = (own, near, cross)
    pick, used = picks_of(blocks, kept, jnp.zeros((1, 1), F32))
    pick_out[...] = pick
    used_out[...] = jnp.broadcast_to(used, used_out.shape)
    rows_out[...] = dot(pick, jnp.concatenate([side_by_side(ref) for ref in blocks], axis=0)).astype(
        BF16
    )
    turned_out[...] = turned(pick)


def main_body(far, turned_ref, rows_ref, used_ref, own_out, near_out, far_out, cross_out, last_out):
    kept = rows_ref.shape[0]
    tokens = far.shape[0] // 4
    last, _ = picks_of((far,), kept, used_ref[0:1, 0:1])
    last_out[...] = last
    rows = rows_ref[...] + dot(last, side_by_side(far)).astype(BF16)
    result = attend_head(rows)
    put_back(far_out, turned(last), result)
    for n, out in ((1, near_out), (2, cross_out), (0, own_out)):
        put_back(out, turned_ref[n * tokens : (n + 1) * tokens, :], result)


def shared_body(pick_ref, last_ref, turned_ref, own, near, cross, far, own_out, near_out):
    tokens = last_ref.shape[1]
    pick = jnp.concatenate([pick_ref[...], last_ref[...]], axis=1)
    blocks = (own, near, cross, far)
    rows = dot(pick, jnp.concatenate([side_by_side(ref) for ref in blocks], axis=0)).astype(BF16)
    result = attend_head(rows)
    put_back(own_out, turned_ref[0:tokens, :], result)
    put_back(near_out, turned_ref[tokens : 2 * tokens, :], result)


def placed(back, tokens, lanes, outs, sems):
    return [
        pltpu.make_async_copy(
            back.at[n * tokens : (n + 1) * tokens, :], out.at[0, :, lanes], sems.at[n]
        )
        for n, out in enumerate(outs)
    ]


def last_body(steps, *refs):
    backs, (shared_here, shared_there) = refs[: len(steps)], refs[len(steps) : -6]
    outs, shared, sems = refs[-6:-2], refs[-2], refs[-1]
    tokens = outs[0].shape[1]
    me = lax.axis_index("win")
    copies = []
    for n, (back, step) in enumerate(zip(backs, steps)):
        copies += placed(back, tokens, head_lanes(me ^ step), outs, sems.at[n])
    for copy in copies:
        copy.start()
    at_end = jnp.logical_or(me == 0, me == WINDOWS - 1)

    @pl.when(at_end)
    def _():
        shared[...] = shared_there[...]

    @pl.when(jnp.logical_not(at_end))
    def _():
        shared[...] = shared_here[...]

    more = placed(shared, tokens, head_lanes(WINDOWS), outs, sems.at[len(steps)])
    for copy in more:
        copy.start()
    for copy in copies + more:
        copy.wait()


def exchange(array, step):
    return lax.ppermute(array, "win", [(n, n ^ step) for n in range(WINDOWS)])


def along(array, *pairs):
    return lax.ppermute(array, "win", pairs)


def after(array, other):
    return lax.optimization_barrier((array, other))


def shards_by_head(queries, key_vectors, value_vectors, out_grad, keep_mask):
    tokens = queries.shape[1]
    kept = WINDOWS * tokens // 2
    in_hbm = pl.BlockSpec(memory_space=pltpu.HBM)
    block = jax.ShapeDtypeStruct((4 * tokens, HEAD_DIM), BF16)
    rows = jax.ShapeDtypeStruct((kept, 4 * HEAD_DIM), BF16)
    turned_picks = jax.ShapeDtypeStruct((3 * tokens, kept), BF16)
    whole = jax.ShapeDtypeStruct(queries.shape, BF16)

    def picks(windows):
        return jax.ShapeDtypeStruct((kept, windows * tokens), BF16)

    def call(body, out_shape, *operands, flops=0, **specs):
        return pl.pallas_call(
            body,
            out_shape=out_shape,
            cost_estimate=pl.CostEstimate(flops=flops, bytes_accessed=0, transcendentals=0),
            compiler_params=pltpu.CompilerParams(vmem_limit_bytes=VMEM_BYTES),
            **specs,
        )(*operands)

    pinned = [
        pltpu.with_memory_space_constraint(one, pltpu.HBM)
        for one in (queries, key_vectors, value_vectors, out_grad, keep_mask)
    ]

    def pack(*steps):
        return call(
            functools.partial(pack_body, steps),
            [block] * len(steps),
            *pinned,
            in_specs=[in_hbm] * 5,
            scratch_shapes=[
                pltpu.VMEM(keep_mask.shape, keep_mask.dtype),
                pltpu.SemaphoreType.DMA((1 + 4 * len(steps),)),
            ],
        )

    (cross,) = pack(3)
    far, near, own, shared = pack(2, 1, 0, None)
    got_cross = exchange(cross, 3)
    got_far = exchange(far, 2)
    got_near = exchange(near, 1)
    late, got_cross = after(shared, got_cross)
    shared_near = along(shared, (0, 1), (3, 2))
    shared_cross = along(late, (1, 2), (2, 1))
    shared_far = along(shared_near, (1, 2), (2, 1))
    pick, turned_pick, some_rows, used = call(
        early_body,
        [picks(3), turned_picks, rows, jax.ShapeDtypeStruct((8, HEAD_DIM), F32)],
        own,
        got_near,
        got_cross,
        flops=1 << 28,
    )
    own_result, near_result, far_result, cross_result, last = call(
        main_body, [block] * 4 + [picks(1)], got_far, turned_pick, some_rows, used, flops=1 << 29
    )
    back_near = exchange(near_result, 1)
    back_far = exchange(far_result, 2)
    back_cross = exchange(cross_result, 3)
    shared_here, for_near = call(
        shared_body,
        [block] * 2,
        pick,
        last,
        turned_pick,
        shared,
        shared_near,
        shared_cross,
        shared_far,
    )
    shared_there = along(for_near, (1, 0), (2, 3))
    steps = (0, 1, 2, 3)
    return call(
        functools.partial(last_body, steps),
        [whole] * 4,
        own_result,
        back_near,
        back_far,
        back_cross,
        shared_here,
        shared_there,
        out_specs=[in_hbm] * 4,
        scratch_shapes=[
            pltpu.VMEM(block.shape, BF16),
            pltpu.SemaphoreType.DMA((len(steps) + 1, 4)),
        ],
    )


def fold_blocks(step_fn, carried, arrays):
    count = arrays[0].shape[0]
    width = 512 if count % 512 == 0 else count
    blocks = tuple(
        (member.reshape((count // width, width) + member.shape[1:]) for member in arrays)
    )

    def inner_step(state, current):
        return (step_fn(state, current), None)

    result, unused = lax.scan(inner_step, carried, blocks)
    return result


def shards(queries, key_vectors, value_vectors, out_grad, keep_mask):
    win_count = lax.axis_size("win")
    win_index = lax.axis_index("win")
    tok_rows = queries.shape[1]
    feat_dev = queries.shape[2]
    head_count = feat_dev // HEAD_DIM
    slot_rows = tok_rows // win_count
    own_rows = tok_rows // 2
    inv_root = 1.0 / math.sqrt(HEAD_DIM)
    kept_flag = keep_mask[0]
    kept_here = jnp.sum(kept_flag)
    counts = lax.all_gather(kept_here.reshape(1), "win", axis=0, tiled=True)
    starts = jnp.cumsum(counts) - counts
    ends = starts + counts
    start_here = starts[win_index]
    kept_order = jnp.argsort(1 - kept_flag, stable=True)
    kept_rank = jnp.cumsum(kept_flag) - 1
    slot_index = jnp.arange(tok_rows, dtype=jnp.int32)
    target = slot_index // slot_rows
    within = slot_index % slot_rows
    leading = start_here + jnp.mod(target - start_here, win_count)
    global_pos = leading + within * win_count
    send_live = global_pos < start_here + kept_here
    send_rows = kept_order[jnp.clip(global_pos - start_here, 0, tok_rows - 1)]

    def pack(matrix):
        return jnp.where(send_live[:, None], matrix[0][send_rows], jnp.zeros((), matrix.dtype))

    own_index = jnp.arange(own_rows, dtype=jnp.int32)
    wanted = own_index * win_count + win_index
    source = jnp.sum((ends[None, :] <= wanted[:, None]).astype(jnp.int32), axis=1)
    source_start = starts[source]
    source_lead = source_start + jnp.mod(win_index - source_start, win_count)
    recv_rows = source * slot_rows + (wanted - source_lead) // win_count

    def unpack(matrix):
        return matrix[recv_rows]

    back_start = starts[target]
    back_lead = back_start + jnp.mod(win_index - back_start, win_count)
    back_global = back_lead + within * win_count
    back_live = back_global < ends[target]
    back_rows = jnp.clip(back_global // win_count, 0, own_rows - 1)

    def repack(matrix):
        return jnp.where(back_live[:, None], matrix[back_rows], jnp.zeros((), matrix.dtype))

    global_here = start_here + kept_rank
    owner = jnp.mod(global_here, win_count)
    owner_lead = start_here + jnp.mod(owner - start_here, win_count)
    land_rows = jnp.clip(
        owner * slot_rows + (global_here - owner_lead) // win_count, 0, tok_rows - 1
    )

    def place(matrix):
        return jnp.where(kept_flag[:, None] == 1, matrix[land_rows], jnp.zeros((), matrix.dtype))[
            None
        ]

    def heads_view(matrix):
        return matrix.reshape(matrix.shape[0], head_count, HEAD_DIM)

    got_query, got_key, got_value = (
        lax.all_to_all(pack(queries), "win", split_axis=0, concat_axis=0, tiled=True),
        lax.all_to_all(pack(key_vectors), "win", split_axis=0, concat_axis=0, tiled=True),
        lax.all_to_all(pack(value_vectors), "win", split_axis=0, concat_axis=0, tiled=True),
    )
    query_rows = unpack(got_query)
    key_rows = unpack(got_key)
    value_rows = unpack(got_value)
    query_heads = heads_view(query_rows)

    def soft_step(carried, current):
        highest, totals, summed = carried
        block_keys, block_values = current
        scores = (
            jnp.einsum(
                "qhe,khe->hqk",
                query_heads,
                heads_view(block_keys),
                preferred_element_type=jnp.float32,
            )
            * inv_root
        )
        peak_new = jnp.maximum(highest, jnp.max(scores, axis=-1))
        shrink = jnp.exp(highest - peak_new)
        raised = jnp.exp(scores - peak_new[..., None])
        totals = totals * shrink + jnp.sum(raised, axis=-1)
        summed = summed * shrink.T[..., None] + jnp.einsum(
            "hqk,khe->qhe",
            raised.astype(jnp.bfloat16),
            heads_view(block_values),
            preferred_element_type=jnp.float32,
        )
        return (peak_new, totals, summed)

    start_state = (
        jnp.full((head_count, own_rows), -jnp.inf, jnp.float32),
        jnp.zeros((head_count, own_rows), jnp.float32),
        jnp.zeros((own_rows, head_count, HEAD_DIM), jnp.float32),
    )
    highest, totals, summed = fold_blocks(
        soft_step,
        start_state,
        (
            lax.all_gather(key_rows, "win", axis=0, tiled=True),
            lax.all_gather(value_rows, "win", axis=0, tiled=True),
        ),
    )
    log_total = highest + jnp.log(totals)
    attended = (summed / totals.T[..., None]).astype(jnp.bfloat16)
    grad_rows = unpack(
        lax.all_to_all(pack(out_grad), "win", split_axis=0, concat_axis=0, tiled=True)
    )
    grad_heads = heads_view(grad_rows)
    inner = jnp.sum(grad_heads.astype(jnp.float32) * attended.astype(jnp.float32), axis=-1).T

    def query_step(carried, current):
        block_keys, block_values = current
        key_heads = heads_view(block_keys)
        scores = (
            jnp.einsum("qhe,khe->hqk", query_heads, key_heads, preferred_element_type=jnp.float32)
            * inv_root
        )
        weights = jnp.exp(scores - log_total[..., None]).astype(jnp.bfloat16)
        grad_scores = jnp.einsum(
            "qhe,khe->hqk", grad_heads, heads_view(block_values), preferred_element_type=jnp.float32
        )
        grad_logits = (
            weights.astype(jnp.float32) * (grad_scores - inner[..., None]) * inv_root
        ).astype(jnp.bfloat16)
        return carried + jnp.einsum(
            "hqk,khe->qhe", grad_logits, key_heads, preferred_element_type=jnp.float32
        )

    query_zero = jnp.zeros((own_rows, head_count, HEAD_DIM), jnp.float32)
    grad_query = fold_blocks(
        query_step,
        query_zero,
        (
            lax.all_gather(key_rows, "win", axis=0, tiled=True),
            lax.all_gather(value_rows, "win", axis=0, tiled=True),
        ),
    )
    all_log, all_inner = (
        lax.all_gather(log_total.T, "win", axis=0, tiled=True),
        lax.all_gather(inner.T, "win", axis=0, tiled=True),
    )
    own_key_heads = heads_view(key_rows)
    own_value_heads = heads_view(value_rows)

    def key_step(carried, current):
        key_total, value_total = carried
        block_queries, block_grads, block_log, block_inner = current
        query_block = heads_view(block_queries)
        grad_block = heads_view(block_grads)
        scores = (
            jnp.einsum(
                "khe,qhe->hkq", own_key_heads, query_block, preferred_element_type=jnp.float32
            )
            * inv_root
        )
        weights = jnp.exp(scores - block_log.T[:, None, :]).astype(jnp.bfloat16)
        value_total = value_total + jnp.einsum(
            "hkq,qhe->khe", weights, grad_block, preferred_element_type=jnp.float32
        )
        grad_scores = jnp.einsum(
            "khe,qhe->hkq", own_value_heads, grad_block, preferred_element_type=jnp.float32
        )
        grad_logits = (
            weights.astype(jnp.float32) * (grad_scores - block_inner.T[:, None, :]) * inv_root
        ).astype(jnp.bfloat16)
        key_total = key_total + jnp.einsum(
            "hkq,qhe->khe", grad_logits, query_block, preferred_element_type=jnp.float32
        )
        return (key_total, value_total)

    key_rows_count = key_rows.shape[0]
    empty_grads = jnp.zeros((key_rows_count, head_count, HEAD_DIM), jnp.float32)
    key_total, value_total = fold_blocks(
        key_step,
        (empty_grads, empty_grads),
        (
            lax.all_gather(query_rows, "win", axis=0, tiled=True),
            lax.all_gather(grad_rows, "win", axis=0, tiled=True),
            all_log,
            all_inner,
        ),
    )
    grad_key = key_total.reshape(key_rows_count, feat_dev).astype(jnp.bfloat16)
    grad_value = value_total.reshape(key_rows_count, feat_dev).astype(jnp.bfloat16)
    attended_flat = attended.reshape(own_rows, feat_dev)
    grad_query_flat = grad_query.reshape(own_rows, feat_dev).astype(jnp.bfloat16)
    back_attended, back_query, back_key, back_value = (
        lax.all_to_all(repack(attended_flat), "win", split_axis=0, concat_axis=0, tiled=True),
        lax.all_to_all(repack(grad_query_flat), "win", split_axis=0, concat_axis=0, tiled=True),
        lax.all_to_all(repack(grad_key), "win", split_axis=0, concat_axis=0, tiled=True),
        lax.all_to_all(repack(grad_value), "win", split_axis=0, concat_axis=0, tiled=True),
    )
    grad_key_out = place(back_key)
    grad_value_out = place(back_value)
    return (place(back_attended), place(back_query), grad_key_out, grad_value_out)


def by_plan(queries, key_vectors, value_vectors, out_grad, keep_mask):
    tokens, feat_dev = queries.shape[1:]
    dealt = lax.axis_size("win") == WINDOWS and feat_dev == (WINDOWS + 1) * HEAD_DIM
    run = shards_by_head if dealt and tokens == HEAD_DIM else shards
    return run(queries, key_vectors, value_vectors, out_grad, keep_mask)


def solution(mesh):
    placed = (
        P(("groups", "samp"), "win", "head"),
        P(("groups", "samp"), "win", "head"),
        P(("groups", "samp"), "win", "head"),
        P(("groups", "samp"), "win", "head"),
        P(("groups", "samp"), "win"),
    )
    return jax.shard_map(
        by_plan,
        mesh=mesh,
        in_specs=placed,
        out_specs=(
            P(("groups", "samp"), "win", "head"),
            P(("groups", "samp"), "win", "head"),
            P(("groups", "samp"), "win", "head"),
            P(("groups", "samp"), "win", "head"),
        ),
        check_vma=False,
    )
```

```python
import functools
import math

import jax
import jax.numpy as jnp
from jax import lax
from jax.experimental import pallas as pl
from jax.experimental.pallas import tpu as pltpu
from jax.sharding import PartitionSpec as P

HEAD_DIM = 128
TILE_ROWS = 16
WINDOWS = 4
DROPPED = 64.0
VMEM_BYTES = 16 << 20
BF16 = jnp.bfloat16
F32 = jnp.float32


def dot(left, right, left_dim=1, right_dim=0):
    return lax.dot_general(
        left, right, (((left_dim,), (right_dim,)), ((), ())), preferred_element_type=F32
    )


def attend_head(rows, needed=None):
    inv_root = 1.0 / math.sqrt(HEAD_DIM)
    needed = rows.shape[0] if needed is None else needed
    q, k, v, g = (rows[:, n * HEAD_DIM : (n + 1) * HEAD_DIM] for n in range(4))
    scores = dot(q, k, 1, 1) * inv_root
    grad_scores = dot(g, v, 1, 1)
    raised = jnp.exp(scores - jnp.max(scores, axis=1, keepdims=True))
    share = 1.0 / jnp.sum(raised, axis=1, keepdims=True)
    inner = jnp.sum(raised * grad_scores, axis=1, keepdims=True) * share
    weights = raised * share
    grad_logits = (weights * ((grad_scores - inner) * inv_root)).astype(BF16)
    weights = weights.astype(BF16)
    attended = (dot(raised[:needed].astype(BF16), v) * share[:needed]).astype(BF16)
    grad_q = dot(grad_logits[:needed], k).astype(BF16)
    grad_k = dot(grad_logits[:, :needed], q, 0, 0).astype(BF16)
    grad_v = dot(weights[:, :needed], g, 0, 0).astype(BF16)
    return jnp.concatenate([attended, grad_q, grad_k, grad_v], axis=1)


def side_by_side(ref):
    tokens = ref.shape[0] // 4
    return jnp.concatenate([ref[n * tokens : (n + 1) * tokens, :] for n in range(4)], axis=1)


def picks_of(blocks, kept, before):
    tokens = blocks[0].shape[0] // 4
    lead = (lax.broadcasted_iota(jnp.int32, (TILE_ROWS, HEAD_DIM), 1) == 0).astype(BF16)
    upto = (
        lax.broadcasted_iota(jnp.int32, (tokens, tokens), 0)
        <= lax.broadcasted_iota(jnp.int32, (tokens, tokens), 1)
    ).astype(BF16)
    slot = lax.broadcasted_iota(jnp.int32, (kept, tokens), 0).astype(F32)
    picks = []
    for block in blocks:
        live = dot(lead, block[0:tokens, :], 1, 1) < 0.5 * DROPPED
        rank = dot(live.astype(F32).astype(BF16), upto)[0:1]
        place = jnp.where(live[0:1], rank + (before - 1.0), -1.0)
        picks.append((slot == place).astype(F32).astype(BF16))
        before = before + rank[:, tokens - 1 : tokens]
    return jnp.concatenate(picks, axis=1), before


def put_back(out, picked, result):
    tokens = picked.shape[0]
    rows = dot(picked, result).astype(BF16)
    for n in range(4):
        out[n * tokens : (n + 1) * tokens, :] = rows[:, n * HEAD_DIM : (n + 1) * HEAD_DIM]


def head_lanes(head):
    if isinstance(head, int):
        return pl.ds(head * HEAD_DIM, HEAD_DIM)
    return pl.ds(pl.multiple_of(head * HEAD_DIM, HEAD_DIM), HEAD_DIM)


def pack_body(steps, q_ref, k_ref, v_ref, g_ref, mask_ref, *refs):
    outs, (mask_here, sems) = refs[:-2], refs[-2:]
    tokens = mask_ref.shape[1]
    me = lax.axis_index("win")
    copies = [pltpu.make_async_copy(mask_ref, mask_here, sems.at[0])]
    for out, step in zip(outs, steps):
        lanes = head_lanes(WINDOWS if step is None else me ^ step)
        for n, ref in enumerate((q_ref, k_ref, v_ref, g_ref)):
            copies.append(
                pltpu.make_async_copy(
                    ref.at[0, :, lanes],
                    out.at[n * tokens : (n + 1) * tokens, :],
                    sems.at[len(copies)],
                )
            )
    for copy in copies:
        copy.start()
    copies[0].wait()
    live = jnp.broadcast_to(mask_here[...].astype(F32), (TILE_ROWS, tokens)).astype(BF16)
    share = jnp.full((TILE_ROWS, HEAD_DIM), 1.0 / TILE_ROWS, BF16)
    keep = dot(live, share, 0, 0)
    mark = (1.0 - keep) * DROPPED
    for copy in copies[1:]:
        copy.wait()
    for out, step in zip(outs, steps):
        if step is not None:
            out[0:tokens, :] = (out[0:tokens, :].astype(F32) * keep + mark).astype(BF16)


def turned(pick):
    kept = pick.shape[0]
    unit = (
        lax.broadcasted_iota(jnp.int32, (kept, kept), 0)
        == lax.broadcasted_iota(jnp.int32, (kept, kept), 1)
    ).astype(F32).astype(BF16)
    return dot(pick, unit, 0, 0).astype(BF16)


def early_body(own, cross, pick_out, turned_out, rows_out, used_out):
    kept = pick_out.shape[0]
    blocks = (own, cross)
    pick, used = picks_of(blocks, kept, jnp.zeros((1, 1), F32))
    pick_out[...] = pick
    used_out[...] = jnp.broadcast_to(used, used_out.shape)
    rows_out[...] = dot(pick, jnp.concatenate([side_by_side(ref) for ref in blocks], axis=0)).astype(
        BF16
    )
    turned_out[...] = turned(pick)


def main_body(
    far,
    near,
    turned_ref,
    rows_ref,
    used_ref,
    own_out,
    near_out,
    far_out,
    cross_out,
    last_out,
    turned_out,
):
    kept = rows_ref.shape[0]
    tokens = far.shape[0] // 4
    last, _ = picks_of((near, far), kept, used_ref[0:1, 0:1])
    last_out[...] = last
    blocks = jnp.concatenate([side_by_side(near), side_by_side(far)], axis=0)
    rows = rows_ref[...] + dot(last, blocks).astype(BF16)
    turned_last = turned(last)
    turned_out[...] = turned_last
    result = attend_head(rows)
    put_back(near_out, turned_last[0:tokens, :], result)
    put_back(far_out, turned_last[tokens:, :], result)
    for n, out in ((1, cross_out), (0, own_out)):
        put_back(out, turned_ref[n * tokens : (n + 1) * tokens, :], result)


def shared_body(pick_ref, last_ref, turned_ref, turned_last_ref, own, cross, near, far, own_out, near_out):
    tokens = last_ref.shape[1] // 2
    pick = jnp.concatenate([pick_ref[...], last_ref[...]], axis=1)
    blocks = (own, cross, near, far)
    rows = dot(pick, jnp.concatenate([side_by_side(ref) for ref in blocks], axis=0)).astype(BF16)
    result = attend_head(rows)
    put_back(own_out, turned_ref[0:tokens, :], result)
    put_back(near_out, turned_last_ref[0:tokens, :], result)


def placed(back, tokens, lanes, outs, sems):
    return [
        pltpu.make_async_copy(
            back.at[n * tokens : (n + 1) * tokens, :], out.at[0, :, lanes], sems.at[n]
        )
        for n, out in enumerate(outs)
    ]


def last_body(steps, *refs):
    backs, (shared_here, shared_there) = refs[: len(steps)], refs[len(steps) : -6]
    outs, shared, sems = refs[-6:-2], refs[-2], refs[-1]
    tokens = outs[0].shape[1]
    me = lax.axis_index("win")
    copies = []
    for n, (back, step) in enumerate(zip(backs, steps)):
        copies += placed(back, tokens, head_lanes(me ^ step), outs, sems.at[n])
    for copy in copies:
        copy.start()
    at_end = jnp.logical_or(me == 0, me == WINDOWS - 1)

    @pl.when(at_end)
    def _():
        shared[...] = shared_there[...]

    @pl.when(jnp.logical_not(at_end))
    def _():
        shared[...] = shared_here[...]

    more = placed(shared, tokens, head_lanes(WINDOWS), outs, sems.at[len(steps)])
    for copy in more:
        copy.start()
    for copy in copies + more:
        copy.wait()


def exchange(array, step):
    return lax.ppermute(array, "win", [(n, n ^ step) for n in range(WINDOWS)])


def along(array, *pairs):
    return lax.ppermute(array, "win", pairs)


def after(array, other):
    return lax.optimization_barrier((array, other))


def shards_by_head(queries, key_vectors, value_vectors, out_grad, keep_mask):
    tokens = queries.shape[1]
    kept = WINDOWS * tokens // 2
    in_hbm = pl.BlockSpec(memory_space=pltpu.HBM)
    block = jax.ShapeDtypeStruct((4 * tokens, HEAD_DIM), BF16)
    rows = jax.ShapeDtypeStruct((kept, 4 * HEAD_DIM), BF16)
    turned_picks = jax.ShapeDtypeStruct((2 * tokens, kept), BF16)
    whole = jax.ShapeDtypeStruct(queries.shape, BF16)

    def picks(windows):
        return jax.ShapeDtypeStruct((kept, windows * tokens), BF16)

    def call(body, out_shape, *operands, flops=0, **specs):
        return pl.pallas_call(
            body,
            out_shape=out_shape,
            cost_estimate=pl.CostEstimate(flops=flops, bytes_accessed=0, transcendentals=0),
            compiler_params=pltpu.CompilerParams(vmem_limit_bytes=VMEM_BYTES),
            **specs,
        )(*operands)

    pinned = [
        pltpu.with_memory_space_constraint(one, pltpu.HBM)
        for one in (queries, key_vectors, value_vectors, out_grad, keep_mask)
    ]

    def pack(*steps):
        return call(
            functools.partial(pack_body, steps),
            [block] * len(steps),
            *pinned,
            in_specs=[in_hbm] * 5,
            scratch_shapes=[
                pltpu.VMEM(keep_mask.shape, keep_mask.dtype),
                pltpu.SemaphoreType.DMA((1 + 4 * len(steps),)),
            ],
        )

    (cross,) = pack(3)
    far, near, own, shared = pack(2, 1, 0, None)
    got_cross = exchange(cross, 3)
    got_far = exchange(far, 2)
    got_near = exchange(near, 1)
    late, got_cross = after(shared, got_cross)
    shared_near = along(shared, (0, 1), (3, 2))
    shared_cross = along(late, (1, 2), (2, 1))
    shared_far = along(shared_near, (1, 2), (2, 1))
    pick, turned_pick, some_rows, used = call(
        early_body,
        [picks(2), turned_picks, rows, jax.ShapeDtypeStruct((8, HEAD_DIM), F32)],
        own,
        got_cross,
        flops=1 << 28,
    )
    own_result, near_result, far_result, cross_result, last, turned_last = call(
        main_body,
        [block] * 4 + [picks(2), turned_picks],
        got_far,
        got_near,
        turned_pick,
        some_rows,
        used,
        flops=1 << 29,
    )
    back_near = exchange(near_result, 1)
    back_far = exchange(far_result, 2)
    back_cross = exchange(cross_result, 3)
    shared_here, for_near = call(
        shared_body,
        [block] * 2,
        pick,
        last,
        turned_pick,
        turned_last,
        shared,
        shared_cross,
        shared_near,
        shared_far,
    )
    shared_there = along(for_near, (1, 0), (2, 3))
    steps = (0, 1, 2, 3)
    return call(
        functools.partial(last_body, steps),
        [whole] * 4,
        own_result,
        back_near,
        back_far,
        back_cross,
        shared_here,
        shared_there,
        out_specs=[in_hbm] * 4,
        scratch_shapes=[
            pltpu.VMEM(block.shape, BF16),
            pltpu.SemaphoreType.DMA((len(steps) + 1, 4)),
        ],
    )


def fold_blocks(step_fn, carried, arrays):
    count = arrays[0].shape[0]
    width = 512 if count % 512 == 0 else count
    blocks = tuple(
        (member.reshape((count // width, width) + member.shape[1:]) for member in arrays)
    )

    def inner_step(state, current):
        return (step_fn(state, current), None)

    result, unused = lax.scan(inner_step, carried, blocks)
    return result


def shards(queries, key_vectors, value_vectors, out_grad, keep_mask):
    win_count = lax.axis_size("win")
    win_index = lax.axis_index("win")
    tok_rows = queries.shape[1]
    feat_dev = queries.shape[2]
    head_count = feat_dev // HEAD_DIM
    slot_rows = tok_rows // win_count
    own_rows = tok_rows // 2
    inv_root = 1.0 / math.sqrt(HEAD_DIM)
    kept_flag = keep_mask[0]
    kept_here = jnp.sum(kept_flag)
    counts = lax.all_gather(kept_here.reshape(1), "win", axis=0, tiled=True)
    starts = jnp.cumsum(counts) - counts
    ends = starts + counts
    start_here = starts[win_index]
    kept_order = jnp.argsort(1 - kept_flag, stable=True)
    kept_rank = jnp.cumsum(kept_flag) - 1
    slot_index = jnp.arange(tok_rows, dtype=jnp.int32)
    target = slot_index // slot_rows
    within = slot_index % slot_rows
    leading = start_here + jnp.mod(target - start_here, win_count)
    global_pos = leading + within * win_count
    send_live = global_pos < start_here + kept_here
    send_rows = kept_order[jnp.clip(global_pos - start_here, 0, tok_rows - 1)]

    def pack(matrix):
        return jnp.where(send_live[:, None], matrix[0][send_rows], jnp.zeros((), matrix.dtype))

    own_index = jnp.arange(own_rows, dtype=jnp.int32)
    wanted = own_index * win_count + win_index
    source = jnp.sum((ends[None, :] <= wanted[:, None]).astype(jnp.int32), axis=1)
    source_start = starts[source]
    source_lead = source_start + jnp.mod(win_index - source_start, win_count)
    recv_rows = source * slot_rows + (wanted - source_lead) // win_count

    def unpack(matrix):
        return matrix[recv_rows]

    back_start = starts[target]
    back_lead = back_start + jnp.mod(win_index - back_start, win_count)
    back_global = back_lead + within * win_count
    back_live = back_global < ends[target]
    back_rows = jnp.clip(back_global // win_count, 0, own_rows - 1)

    def repack(matrix):
        return jnp.where(back_live[:, None], matrix[back_rows], jnp.zeros((), matrix.dtype))

    global_here = start_here + kept_rank
    owner = jnp.mod(global_here, win_count)
    owner_lead = start_here + jnp.mod(owner - start_here, win_count)
    land_rows = jnp.clip(
        owner * slot_rows + (global_here - owner_lead) // win_count, 0, tok_rows - 1
    )

    def place(matrix):
        return jnp.where(kept_flag[:, None] == 1, matrix[land_rows], jnp.zeros((), matrix.dtype))[
            None
        ]

    def heads_view(matrix):
        return matrix.reshape(matrix.shape[0], head_count, HEAD_DIM)

    got_query, got_key, got_value = (
        lax.all_to_all(pack(queries), "win", split_axis=0, concat_axis=0, tiled=True),
        lax.all_to_all(pack(key_vectors), "win", split_axis=0, concat_axis=0, tiled=True),
        lax.all_to_all(pack(value_vectors), "win", split_axis=0, concat_axis=0, tiled=True),
    )
    query_rows = unpack(got_query)
    key_rows = unpack(got_key)
    value_rows = unpack(got_value)
    query_heads = heads_view(query_rows)

    def soft_step(carried, current):
        highest, totals, summed = carried
        block_keys, block_values = current
        scores = (
            jnp.einsum(
                "qhe,khe->hqk",
                query_heads,
                heads_view(block_keys),
                preferred_element_type=jnp.float32,
            )
            * inv_root
        )
        peak_new = jnp.maximum(highest, jnp.max(scores, axis=-1))
        shrink = jnp.exp(highest - peak_new)
        raised = jnp.exp(scores - peak_new[..., None])
        totals = totals * shrink + jnp.sum(raised, axis=-1)
        summed = summed * shrink.T[..., None] + jnp.einsum(
            "hqk,khe->qhe",
            raised.astype(jnp.bfloat16),
            heads_view(block_values),
            preferred_element_type=jnp.float32,
        )
        return (peak_new, totals, summed)

    start_state = (
        jnp.full((head_count, own_rows), -jnp.inf, jnp.float32),
        jnp.zeros((head_count, own_rows), jnp.float32),
        jnp.zeros((own_rows, head_count, HEAD_DIM), jnp.float32),
    )
    highest, totals, summed = fold_blocks(
        soft_step,
        start_state,
        (
            lax.all_gather(key_rows, "win", axis=0, tiled=True),
            lax.all_gather(value_rows, "win", axis=0, tiled=True),
        ),
    )
    log_total = highest + jnp.log(totals)
    attended = (summed / totals.T[..., None]).astype(jnp.bfloat16)
    grad_rows = unpack(
        lax.all_to_all(pack(out_grad), "win", split_axis=0, concat_axis=0, tiled=True)
    )
    grad_heads = heads_view(grad_rows)
    inner = jnp.sum(grad_heads.astype(jnp.float32) * attended.astype(jnp.float32), axis=-1).T

    def query_step(carried, current):
        block_keys, block_values = current
        key_heads = heads_view(block_keys)
        scores = (
            jnp.einsum("qhe,khe->hqk", query_heads, key_heads, preferred_element_type=jnp.float32)
            * inv_root
        )
        weights = jnp.exp(scores - log_total[..., None]).astype(jnp.bfloat16)
        grad_scores = jnp.einsum(
            "qhe,khe->hqk", grad_heads, heads_view(block_values), preferred_element_type=jnp.float32
        )
        grad_logits = (
            weights.astype(jnp.float32) * (grad_scores - inner[..., None]) * inv_root
        ).astype(jnp.bfloat16)
        return carried + jnp.einsum(
            "hqk,khe->qhe", grad_logits, key_heads, preferred_element_type=jnp.float32
        )

    query_zero = jnp.zeros((own_rows, head_count, HEAD_DIM), jnp.float32)
    grad_query = fold_blocks(
        query_step,
        query_zero,
        (
            lax.all_gather(key_rows, "win", axis=0, tiled=True),
            lax.all_gather(value_rows, "win", axis=0, tiled=True),
        ),
    )
    all_log, all_inner = (
        lax.all_gather(log_total.T, "win", axis=0, tiled=True),
        lax.all_gather(inner.T, "win", axis=0, tiled=True),
    )
    own_key_heads = heads_view(key_rows)
    own_value_heads = heads_view(value_rows)

    def key_step(carried, current):
        key_total, value_total = carried
        block_queries, block_grads, block_log, block_inner = current
        query_block = heads_view(block_queries)
        grad_block = heads_view(block_grads)
        scores = (
            jnp.einsum(
                "khe,qhe->hkq", own_key_heads, query_block, preferred_element_type=jnp.float32
            )
            * inv_root
        )
        weights = jnp.exp(scores - block_log.T[:, None, :]).astype(jnp.bfloat16)
        value_total = value_total + jnp.einsum(
            "hkq,qhe->khe", weights, grad_block, preferred_element_type=jnp.float32
        )
        grad_scores = jnp.einsum(
            "khe,qhe->hkq", own_value_heads, grad_block, preferred_element_type=jnp.float32
        )
        grad_logits = (
            weights.astype(jnp.float32) * (grad_scores - block_inner.T[:, None, :]) * inv_root
        ).astype(jnp.bfloat16)
        key_total = key_total + jnp.einsum(
            "hkq,qhe->khe", grad_logits, query_block, preferred_element_type=jnp.float32
        )
        return (key_total, value_total)

    key_rows_count = key_rows.shape[0]
    empty_grads = jnp.zeros((key_rows_count, head_count, HEAD_DIM), jnp.float32)
    key_total, value_total = fold_blocks(
        key_step,
        (empty_grads, empty_grads),
        (
            lax.all_gather(query_rows, "win", axis=0, tiled=True),
            lax.all_gather(grad_rows, "win", axis=0, tiled=True),
            all_log,
            all_inner,
        ),
    )
    grad_key = key_total.reshape(key_rows_count, feat_dev).astype(jnp.bfloat16)
    grad_value = value_total.reshape(key_rows_count, feat_dev).astype(jnp.bfloat16)
    attended_flat = attended.reshape(own_rows, feat_dev)
    grad_query_flat = grad_query.reshape(own_rows, feat_dev).astype(jnp.bfloat16)
    back_attended, back_query, back_key, back_value = (
        lax.all_to_all(repack(attended_flat), "win", split_axis=0, concat_axis=0, tiled=True),
        lax.all_to_all(repack(grad_query_flat), "win", split_axis=0, concat_axis=0, tiled=True),
        lax.all_to_all(repack(grad_key), "win", split_axis=0, concat_axis=0, tiled=True),
        lax.all_to_all(repack(grad_value), "win", split_axis=0, concat_axis=0, tiled=True),
    )
    grad_key_out = place(back_key)
    grad_value_out = place(back_value)
    return (place(back_attended), place(back_query), grad_key_out, grad_value_out)


def by_plan(queries, key_vectors, value_vectors, out_grad, keep_mask):
    tokens, feat_dev = queries.shape[1:]
    dealt = lax.axis_size("win") == WINDOWS and feat_dev == (WINDOWS + 1) * HEAD_DIM
    run = shards_by_head if dealt and tokens == HEAD_DIM else shards
    return run(queries, key_vectors, value_vectors, out_grad, keep_mask)


def solution(mesh):
    placed = (
        P(("groups", "samp"), "win", "head"),
        P(("groups", "samp"), "win", "head"),
        P(("groups", "samp"), "win", "head"),
        P(("groups", "samp"), "win", "head"),
        P(("groups", "samp"), "win"),
    )
    return jax.shard_map(
        by_plan,
        mesh=mesh,
        in_specs=placed,
        out_specs=(
            P(("groups", "samp"), "win", "head"),
            P(("groups", "samp"), "win", "head"),
            P(("groups", "samp"), "win", "head"),
            P(("groups", "samp"), "win", "head"),
        ),
        check_vma=False,
    )
```

```python
import functools
import math

import jax
import jax.numpy as jnp
from jax import lax
from jax.experimental import pallas as pl
from jax.experimental.pallas import tpu as pltpu
from jax.sharding import PartitionSpec as P

HEAD_DIM = 128
TILE_ROWS = 16
WINDOWS = 4
DROPPED = 64.0
VMEM_BYTES = 16 << 20
BF16 = jnp.bfloat16
F32 = jnp.float32


def dot(left, right, left_dim=1, right_dim=0):
    return lax.dot_general(
        left, right, (((left_dim,), (right_dim,)), ((), ())), preferred_element_type=F32
    )


def attend_head(rows, needed=None):
    inv_root = 1.0 / math.sqrt(HEAD_DIM)
    needed = rows.shape[0] if needed is None else needed
    q, k, v, g = (rows[:, n * HEAD_DIM : (n + 1) * HEAD_DIM] for n in range(4))
    scores = dot(q, k, 1, 1) * inv_root
    grad_scores = dot(g, v, 1, 1)
    raised = jnp.exp(scores - jnp.max(scores, axis=1, keepdims=True))
    share = 1.0 / jnp.sum(raised, axis=1, keepdims=True)
    inner = jnp.sum(raised * grad_scores, axis=1, keepdims=True) * share
    weights = raised * share
    grad_logits = (weights * ((grad_scores - inner) * inv_root)).astype(BF16)
    weights = weights.astype(BF16)
    attended = (dot(raised[:needed].astype(BF16), v) * share[:needed]).astype(BF16)
    grad_q = dot(grad_logits[:needed], k).astype(BF16)
    grad_k = dot(grad_logits[:, :needed], q, 0, 0).astype(BF16)
    grad_v = dot(weights[:, :needed], g, 0, 0).astype(BF16)
    return jnp.concatenate([attended, grad_q, grad_k, grad_v], axis=1)


def side_by_side(ref):
    tokens = ref.shape[0] // 4
    return jnp.concatenate([ref[n * tokens : (n + 1) * tokens, :] for n in range(4)], axis=1)


def picks_of(blocks, kept, before):
    tokens = blocks[0].shape[0] // 4
    lead = (lax.broadcasted_iota(jnp.int32, (TILE_ROWS, HEAD_DIM), 1) == 0).astype(BF16)
    upto = (
        lax.broadcasted_iota(jnp.int32, (tokens, tokens), 0)
        <= lax.broadcasted_iota(jnp.int32, (tokens, tokens), 1)
    ).astype(BF16)
    slot = lax.broadcasted_iota(jnp.int32, (kept, tokens), 0).astype(F32)
    picks = []
    for block in blocks:
        live = dot(lead, block[0:tokens, :], 1, 1) < 0.5 * DROPPED
        rank = dot(live.astype(F32).astype(BF16), upto)[0:1]
        place = jnp.where(live[0:1], rank + (before - 1.0), -1.0)
        picks.append((slot == place).astype(F32).astype(BF16))
        before = before + rank[:, tokens - 1 : tokens]
    return jnp.concatenate(picks, axis=1), before


def put_back(out, picked, result):
    tokens = picked.shape[0]
    rows = dot(picked, result).astype(BF16)
    for n in range(4):
        out[n * tokens : (n + 1) * tokens, :] = rows[:, n * HEAD_DIM : (n + 1) * HEAD_DIM]


def head_lanes(head):
    if isinstance(head, int):
        return pl.ds(head * HEAD_DIM, HEAD_DIM)
    return pl.ds(pl.multiple_of(head * HEAD_DIM, HEAD_DIM), HEAD_DIM)


def pack_body(steps, q_ref, k_ref, v_ref, g_ref, mask_ref, *refs):
    outs, (mask_here, sems) = refs[:-2], refs[-2:]
    tokens = mask_ref.shape[1]
    me = lax.axis_index("win")
    copies = [pltpu.make_async_copy(mask_ref, mask_here, sems.at[0])]
    for out, step in zip(outs, steps):
        lanes = head_lanes(WINDOWS if step is None else me ^ step)
        for n, ref in enumerate((q_ref, k_ref, v_ref, g_ref)):
            copies.append(
                pltpu.make_async_copy(
                    ref.at[0, :, lanes],
                    out.at[n * tokens : (n + 1) * tokens, :],
                    sems.at[len(copies)],
                )
            )
    for copy in copies:
        copy.start()
    copies[0].wait()
    live = jnp.broadcast_to(mask_here[...].astype(F32), (TILE_ROWS, tokens)).astype(BF16)
    share = jnp.full((TILE_ROWS, HEAD_DIM), 1.0 / TILE_ROWS, BF16)
    keep = dot(live, share, 0, 0)
    mark = (1.0 - keep) * DROPPED
    for copy in copies[1:]:
        copy.wait()
    for out, step in zip(outs, steps):
        if step is not None:
            out[0:tokens, :] = (out[0:tokens, :].astype(F32) * keep + mark).astype(BF16)


def turned(pick):
    kept = pick.shape[0]
    unit = (
        lax.broadcasted_iota(jnp.int32, (kept, kept), 0)
        == lax.broadcasted_iota(jnp.int32, (kept, kept), 1)
    ).astype(F32).astype(BF16)
    return dot(pick, unit, 0, 0).astype(BF16)


def early_body(own, near, cross, pick_out, turned_out, rows_out, used_out):
    kept = pick_out.shape[0]
    blocks = (own, near, cross)
    pick, used = picks_of(blocks, kept, jnp.zeros((1, 1), F32))
    pick_out[...] = pick
    used_out[...] = jnp.broadcast_to(used, used_out.shape)
    rows_out[...] = dot(pick, jnp.concatenate([side_by_side(ref) for ref in blocks], axis=0)).astype(
        BF16
    )
    turned_out[...] = turned(pick)


def main_body(far, turned_ref, rows_ref, used_ref, own_out, near_out, far_out, cross_out, last_out):
    kept = rows_ref.shape[0]
    tokens = far.shape[0] // 4
    last, _ = picks_of((far,), kept, used_ref[0:1, 0:1])
    last_out[...] = last
    rows = rows_ref[...] + dot(last, side_by_side(far)).astype(BF16)
    result = attend_head(rows)
    put_back(far_out, turned(last), result)
    for n, out in ((1, near_out), (2, cross_out), (0, own_out)):
        put_back(out, turned_ref[n * tokens : (n + 1) * tokens, :], result)


def shared_body(pick_ref, last_ref, turned_ref, own, near, cross, far, own_out, near_out):
    tokens = last_ref.shape[1]
    pick = jnp.concatenate([pick_ref[...], last_ref[...]], axis=1)
    blocks = (own, near, cross, far)
    rows = dot(pick, jnp.concatenate([side_by_side(ref) for ref in blocks], axis=0)).astype(BF16)
    result = attend_head(rows)
    put_back(own_out, turned_ref[0:tokens, :], result)
    put_back(near_out, turned_ref[tokens : 2 * tokens, :], result)


def placed(back, tokens, lanes, outs, sems):
    return [
        pltpu.make_async_copy(
            back.at[n * tokens : (n + 1) * tokens, :], out.at[0, :, lanes], sems.at[n]
        )
        for n, out in enumerate(outs)
    ]


def last_body(steps, *refs):
    backs, (shared_here, shared_there) = refs[: len(steps)], refs[len(steps) : -6]
    outs, shared, sems = refs[-6:-2], refs[-2], refs[-1]
    tokens = outs[0].shape[1]
    me = lax.axis_index("win")
    copies = []
    for n, (back, step) in enumerate(zip(backs, steps)):
        copies += placed(back, tokens, head_lanes(me ^ step), outs, sems.at[n])
    for copy in copies:
        copy.start()
    at_end = jnp.logical_or(me == 0, me == WINDOWS - 1)

    @pl.when(at_end)
    def _():
        shared[...] = shared_there[...]

    @pl.when(jnp.logical_not(at_end))
    def _():
        shared[...] = shared_here[...]

    more = placed(shared, tokens, head_lanes(WINDOWS), outs, sems.at[len(steps)])
    for copy in more:
        copy.start()
    for copy in copies + more:
        copy.wait()


def exchange(array, step):
    return lax.ppermute(array, "win", [(n, n ^ step) for n in range(WINDOWS)])


def along(array, *pairs):
    return lax.ppermute(array, "win", pairs)


def after(array, other):
    return lax.optimization_barrier((array, other))


def shards_by_head(queries, key_vectors, value_vectors, out_grad, keep_mask):
    tokens = queries.shape[1]
    kept = WINDOWS * tokens // 2
    in_hbm = pl.BlockSpec(memory_space=pltpu.HBM)
    block = jax.ShapeDtypeStruct((4 * tokens, HEAD_DIM), BF16)
    rows = jax.ShapeDtypeStruct((kept, 4 * HEAD_DIM), BF16)
    turned_picks = jax.ShapeDtypeStruct((3 * tokens, kept), BF16)
    whole = jax.ShapeDtypeStruct(queries.shape, BF16)

    def picks(windows):
        return jax.ShapeDtypeStruct((kept, windows * tokens), BF16)

    def call(body, out_shape, *operands, flops=0, **specs):
        return pl.pallas_call(
            body,
            out_shape=out_shape,
            cost_estimate=pl.CostEstimate(flops=flops, bytes_accessed=0, transcendentals=0),
            compiler_params=pltpu.CompilerParams(vmem_limit_bytes=VMEM_BYTES),
            **specs,
        )(*operands)

    pinned = [
        pltpu.with_memory_space_constraint(one, pltpu.HBM)
        for one in (queries, key_vectors, value_vectors, out_grad, keep_mask)
    ]

    def pack(*steps):
        return call(
            functools.partial(pack_body, steps),
            [block] * len(steps),
            *pinned,
            in_specs=[in_hbm] * 5,
            scratch_shapes=[
                pltpu.VMEM(keep_mask.shape, keep_mask.dtype),
                pltpu.SemaphoreType.DMA((1 + 4 * len(steps),)),
            ],
        )

    cross, shared = pack(3, None)
    near, far, own = pack(1, 2, 0)
    got_cross = exchange(cross, 3)
    got_far = exchange(far, 2)
    got_near = exchange(near, 1)
    late, got_cross = after(shared, got_cross)
    shared_near = along(shared, (0, 1), (3, 2))
    shared_cross = along(late, (1, 2), (2, 1))
    shared_far = along(shared_near, (1, 2), (2, 1))
    pick, turned_pick, some_rows, used = call(
        early_body,
        [picks(3), turned_picks, rows, jax.ShapeDtypeStruct((8, HEAD_DIM), F32)],
        own,
        got_near,
        got_cross,
        flops=1 << 28,
    )
    own_result, near_result, far_result, cross_result, last = call(
        main_body, [block] * 4 + [picks(1)], got_far, turned_pick, some_rows, used, flops=1 << 29
    )
    back_near = exchange(near_result, 1)
    back_far = exchange(far_result, 2)
    back_cross = exchange(cross_result, 3)
    shared_here, for_near = call(
        shared_body,
        [block] * 2,
        pick,
        last,
        turned_pick,
        shared,
        shared_near,
        shared_cross,
        shared_far,
    )
    shared_there = along(for_near, (1, 0), (2, 3))
    steps = (0, 1, 2, 3)
    return call(
        functools.partial(last_body, steps),
        [whole] * 4,
        own_result,
        back_near,
        back_far,
        back_cross,
        shared_here,
        shared_there,
        out_specs=[in_hbm] * 4,
        scratch_shapes=[
            pltpu.VMEM(block.shape, BF16),
            pltpu.SemaphoreType.DMA((len(steps) + 1, 4)),
        ],
    )


def fold_blocks(step_fn, carried, arrays):
    count = arrays[0].shape[0]
    width = 512 if count % 512 == 0 else count
    blocks = tuple(
        (member.reshape((count // width, width) + member.shape[1:]) for member in arrays)
    )

    def inner_step(state, current):
        return (step_fn(state, current), None)

    result, unused = lax.scan(inner_step, carried, blocks)
    return result


def shards(queries, key_vectors, value_vectors, out_grad, keep_mask):
    win_count = lax.axis_size("win")
    win_index = lax.axis_index("win")
    tok_rows = queries.shape[1]
    feat_dev = queries.shape[2]
    head_count = feat_dev // HEAD_DIM
    slot_rows = tok_rows // win_count
    own_rows = tok_rows // 2
    inv_root = 1.0 / math.sqrt(HEAD_DIM)
    kept_flag = keep_mask[0]
    kept_here = jnp.sum(kept_flag)
    counts = lax.all_gather(kept_here.reshape(1), "win", axis=0, tiled=True)
    starts = jnp.cumsum(counts) - counts
    ends = starts + counts
    start_here = starts[win_index]
    kept_order = jnp.argsort(1 - kept_flag, stable=True)
    kept_rank = jnp.cumsum(kept_flag) - 1
    slot_index = jnp.arange(tok_rows, dtype=jnp.int32)
    target = slot_index // slot_rows
    within = slot_index % slot_rows
    leading = start_here + jnp.mod(target - start_here, win_count)
    global_pos = leading + within * win_count
    send_live = global_pos < start_here + kept_here
    send_rows = kept_order[jnp.clip(global_pos - start_here, 0, tok_rows - 1)]

    def pack(matrix):
        return jnp.where(send_live[:, None], matrix[0][send_rows], jnp.zeros((), matrix.dtype))

    own_index = jnp.arange(own_rows, dtype=jnp.int32)
    wanted = own_index * win_count + win_index
    source = jnp.sum((ends[None, :] <= wanted[:, None]).astype(jnp.int32), axis=1)
    source_start = starts[source]
    source_lead = source_start + jnp.mod(win_index - source_start, win_count)
    recv_rows = source * slot_rows + (wanted - source_lead) // win_count

    def unpack(matrix):
        return matrix[recv_rows]

    back_start = starts[target]
    back_lead = back_start + jnp.mod(win_index - back_start, win_count)
    back_global = back_lead + within * win_count
    back_live = back_global < ends[target]
    back_rows = jnp.clip(back_global // win_count, 0, own_rows - 1)

    def repack(matrix):
        return jnp.where(back_live[:, None], matrix[back_rows], jnp.zeros((), matrix.dtype))

    global_here = start_here + kept_rank
    owner = jnp.mod(global_here, win_count)
    owner_lead = start_here + jnp.mod(owner - start_here, win_count)
    land_rows = jnp.clip(
        owner * slot_rows + (global_here - owner_lead) // win_count, 0, tok_rows - 1
    )

    def place(matrix):
        return jnp.where(kept_flag[:, None] == 1, matrix[land_rows], jnp.zeros((), matrix.dtype))[
            None
        ]

    def heads_view(matrix):
        return matrix.reshape(matrix.shape[0], head_count, HEAD_DIM)

    got_query, got_key, got_value = (
        lax.all_to_all(pack(queries), "win", split_axis=0, concat_axis=0, tiled=True),
        lax.all_to_all(pack(key_vectors), "win", split_axis=0, concat_axis=0, tiled=True),
        lax.all_to_all(pack(value_vectors), "win", split_axis=0, concat_axis=0, tiled=True),
    )
    query_rows = unpack(got_query)
    key_rows = unpack(got_key)
    value_rows = unpack(got_value)
    query_heads = heads_view(query_rows)

    def soft_step(carried, current):
        highest, totals, summed = carried
        block_keys, block_values = current
        scores = (
            jnp.einsum(
                "qhe,khe->hqk",
                query_heads,
                heads_view(block_keys),
                preferred_element_type=jnp.float32,
            )
            * inv_root
        )
        peak_new = jnp.maximum(highest, jnp.max(scores, axis=-1))
        shrink = jnp.exp(highest - peak_new)
        raised = jnp.exp(scores - peak_new[..., None])
        totals = totals * shrink + jnp.sum(raised, axis=-1)
        summed = summed * shrink.T[..., None] + jnp.einsum(
            "hqk,khe->qhe",
            raised.astype(jnp.bfloat16),
            heads_view(block_values),
            preferred_element_type=jnp.float32,
        )
        return (peak_new, totals, summed)

    start_state = (
        jnp.full((head_count, own_rows), -jnp.inf, jnp.float32),
        jnp.zeros((head_count, own_rows), jnp.float32),
        jnp.zeros((own_rows, head_count, HEAD_DIM), jnp.float32),
    )
    highest, totals, summed = fold_blocks(
        soft_step,
        start_state,
        (
            lax.all_gather(key_rows, "win", axis=0, tiled=True),
            lax.all_gather(value_rows, "win", axis=0, tiled=True),
        ),
    )
    log_total = highest + jnp.log(totals)
    attended = (summed / totals.T[..., None]).astype(jnp.bfloat16)
    grad_rows = unpack(
        lax.all_to_all(pack(out_grad), "win", split_axis=0, concat_axis=0, tiled=True)
    )
    grad_heads = heads_view(grad_rows)
    inner = jnp.sum(grad_heads.astype(jnp.float32) * attended.astype(jnp.float32), axis=-1).T

    def query_step(carried, current):
        block_keys, block_values = current
        key_heads = heads_view(block_keys)
        scores = (
            jnp.einsum("qhe,khe->hqk", query_heads, key_heads, preferred_element_type=jnp.float32)
            * inv_root
        )
        weights = jnp.exp(scores - log_total[..., None]).astype(jnp.bfloat16)
        grad_scores = jnp.einsum(
            "qhe,khe->hqk", grad_heads, heads_view(block_values), preferred_element_type=jnp.float32
        )
        grad_logits = (
            weights.astype(jnp.float32) * (grad_scores - inner[..., None]) * inv_root
        ).astype(jnp.bfloat16)
        return carried + jnp.einsum(
            "hqk,khe->qhe", grad_logits, key_heads, preferred_element_type=jnp.float32
        )

    query_zero = jnp.zeros((own_rows, head_count, HEAD_DIM), jnp.float32)
    grad_query = fold_blocks(
        query_step,
        query_zero,
        (
            lax.all_gather(key_rows, "win", axis=0, tiled=True),
            lax.all_gather(value_rows, "win", axis=0, tiled=True),
        ),
    )
    all_log, all_inner = (
        lax.all_gather(log_total.T, "win", axis=0, tiled=True),
        lax.all_gather(inner.T, "win", axis=0, tiled=True),
    )
    own_key_heads = heads_view(key_rows)
    own_value_heads = heads_view(value_rows)

    def key_step(carried, current):
        key_total, value_total = carried
        block_queries, block_grads, block_log, block_inner = current
        query_block = heads_view(block_queries)
        grad_block = heads_view(block_grads)
        scores = (
            jnp.einsum(
                "khe,qhe->hkq", own_key_heads, query_block, preferred_element_type=jnp.float32
            )
            * inv_root
        )
        weights = jnp.exp(scores - block_log.T[:, None, :]).astype(jnp.bfloat16)
        value_total = value_total + jnp.einsum(
            "hkq,qhe->khe", weights, grad_block, preferred_element_type=jnp.float32
        )
        grad_scores = jnp.einsum(
            "khe,qhe->hkq", own_value_heads, grad_block, preferred_element_type=jnp.float32
        )
        grad_logits = (
            weights.astype(jnp.float32) * (grad_scores - block_inner.T[:, None, :]) * inv_root
        ).astype(jnp.bfloat16)
        key_total = key_total + jnp.einsum(
            "hkq,qhe->khe", grad_logits, query_block, preferred_element_type=jnp.float32
        )
        return (key_total, value_total)

    key_rows_count = key_rows.shape[0]
    empty_grads = jnp.zeros((key_rows_count, head_count, HEAD_DIM), jnp.float32)
    key_total, value_total = fold_blocks(
        key_step,
        (empty_grads, empty_grads),
        (
            lax.all_gather(query_rows, "win", axis=0, tiled=True),
            lax.all_gather(grad_rows, "win", axis=0, tiled=True),
            all_log,
            all_inner,
        ),
    )
    grad_key = key_total.reshape(key_rows_count, feat_dev).astype(jnp.bfloat16)
    grad_value = value_total.reshape(key_rows_count, feat_dev).astype(jnp.bfloat16)
    attended_flat = attended.reshape(own_rows, feat_dev)
    grad_query_flat = grad_query.reshape(own_rows, feat_dev).astype(jnp.bfloat16)
    back_attended, back_query, back_key, back_value = (
        lax.all_to_all(repack(attended_flat), "win", split_axis=0, concat_axis=0, tiled=True),
        lax.all_to_all(repack(grad_query_flat), "win", split_axis=0, concat_axis=0, tiled=True),
        lax.all_to_all(repack(grad_key), "win", split_axis=0, concat_axis=0, tiled=True),
        lax.all_to_all(repack(grad_value), "win", split_axis=0, concat_axis=0, tiled=True),
    )
    grad_key_out = place(back_key)
    grad_value_out = place(back_value)
    return (place(back_attended), place(back_query), grad_key_out, grad_value_out)


def by_plan(queries, key_vectors, value_vectors, out_grad, keep_mask):
    tokens, feat_dev = queries.shape[1:]
    dealt = lax.axis_size("win") == WINDOWS and feat_dev == (WINDOWS + 1) * HEAD_DIM
    run = shards_by_head if dealt and tokens == HEAD_DIM else shards
    return run(queries, key_vectors, value_vectors, out_grad, keep_mask)


def solution(mesh):
    placed = (
        P(("groups", "samp"), "win", "head"),
        P(("groups", "samp"), "win", "head"),
        P(("groups", "samp"), "win", "head"),
        P(("groups", "samp"), "win", "head"),
        P(("groups", "samp"), "win"),
    )
    return jax.shard_map(
        by_plan,
        mesh=mesh,
        in_specs=placed,
        out_specs=(
            P(("groups", "samp"), "win", "head"),
            P(("groups", "samp"), "win", "head"),
            P(("groups", "samp"), "win", "head"),
            P(("groups", "samp"), "win", "head"),
        ),
        check_vma=False,
    )
```
